32 devices in a mesh: samp: 4 (over y, x), proto: 8 (over z, core).
Axes of the slice: x: 2, y: 2, z: 4, core: 2. Of those that a mesh axis runs over, the one named last changes fastest.
Arguments:
- embeddings: bfloat16 [2, 2048, 256], P(None, 'samp'), may hold values from -60 to 60
- prototypes: bfloat16 [4096, 256], P('proto'), may hold values from -12 to 12
Outputs:
- grad_embed: bfloat16 [2, 2048, 256], P(None, 'samp')
- grad_proto: bfloat16 [4096, 256], P('proto')
- loss: float32 [2, 2048], P(None, 'samp')
The draws below stay inside these ranges and needn't reach their ends.
All inputs are finite; a program needn't handle non-finite values.
Results may differ from the reference program's by a relative error of at most 0.001.
The reference program's roundings to bfloat16 on the way count: a program that leaves them out, or rounds other values in their place, can miss the bound.
Values may be sent and summed in bfloat16 or wider, within the bound.
No kernel may reach another device: no remote copies, remote signals or barrier semaphores. Data moves between devices by JAX's collectives and lax.ppermute only.
A program may use at most 64 MiB of HBM per device.

```python
import math
import jax
import jax.numpy as jnp
from jax import lax

D = 256
ITERS = 3
PROTOS = 4096
SAMPLES = 2048


cluster_count = 8


noise_spread = 0.6


def shared_centers(key, alpha_lo, alpha_hi):
    common = jnp.clip(jax.random.normal(jax.random.fold_in(key, 11), (D,), jnp.float32), -4.0, 4.0)
    own_rows = jnp.clip(jax.random.normal(jax.random.fold_in(key, 12), (cluster_count, D), jnp.float32), -4.0, 4.0)
    alpha = jax.random.uniform(jax.random.fold_in(key, 13), (cluster_count, 1), jnp.float32, alpha_lo, alpha_hi)
    return alpha * common[None, :] + own_rows


def sorted_labels(key, count):
    cluster_weights = jax.random.randint(jax.random.fold_in(key, 1), (cluster_count,), 1, 17, jnp.int32)
    bounds = jnp.cumsum(cluster_weights).astype(jnp.int32)
    picks = jax.random.randint(jax.random.fold_in(key, 2), (count,), 0, bounds[-1], jnp.int32)
    labels = jnp.sum((picks[:, None] >= bounds[None, :-1]).astype(jnp.int32), axis=1)
    return jnp.sort(labels).astype(jnp.int32)


def draw_prototypes(key, part):
    centers = shared_centers(key, 1.2, 2.0)
    key = jax.random.fold_in(key, 101)
    labels = sorted_labels(jax.random.fold_in(key, 5), PROTOS)
    own_part = noise_spread * jnp.clip(jax.random.normal(jax.random.fold_in(key, 23), (PROTOS, D), jnp.float32), -4.0, 4.0)
    summed = jnp.take(centers, labels, axis=0) + own_part
    return jnp.clip(summed, -12.0, 12.0).astype(jnp.bfloat16)


def draw_embeddings(key, part):
    centers = shared_centers(key, 1.2, 2.0)
    key = jax.random.fold_in(key, 202)
    labels = sorted_labels(jax.random.fold_in(key, 6), SAMPLES)
    own_part = noise_spread * jnp.clip(jax.random.normal(jax.random.fold_in(key, 23), (2, SAMPLES, D), jnp.float32), -4.0, 4.0)
    row_scale = jnp.exp(jax.random.uniform(jax.random.fold_in(key, 32), (2, SAMPLES, 1), jnp.float32, 0.0, math.log(10.0)))
    summed = jnp.take(centers, labels, axis=0)[None, :, :] + own_part
    return jnp.clip(summed * row_scale, -60.0, 60.0).astype(jnp.bfloat16)


def setup_inputs(seed: int = 0) -> dict:
    key_list = jax.random.split(jax.random.key(seed), 3)
    return {
        "embeddings": draw_embeddings(jax.random.fold_in(key_list[2], 71), 0),
        "prototypes": draw_prototypes(jax.random.fold_in(key_list[2], 71), 0),
    }


EPS_SINK = 0.05
TEMPER = 0.1

def normalize_rows(values):
    as_float = values.astype(jnp.float32)
    inverse = lax.rsqrt(lax.optimization_barrier(jnp.sum(as_float * as_float, axis=-1, keepdims=True)) + 1e-06)
    return (as_float * inverse, inverse)

def project(summed, unit_rows, inverse):
    return (summed - unit_rows * lax.optimization_barrier(jnp.sum(unit_rows * summed, axis=-1, keepdims=True))) * inverse

def reference(embeddings, prototypes):
    unit_emb, inverse_emb = normalize_rows(embeddings)
    unit_proto, inverse_proto = normalize_rows(prototypes)
    emb_wide = lax.optimization_barrier(unit_emb.astype(jnp.bfloat16)).astype(jnp.float32)
    proto_wide = lax.optimization_barrier(unit_proto.astype(jnp.bfloat16)).astype(jnp.float32)
    block_size = math.gcd(PROTOS, 512)
    num_blocks = PROTOS // block_size
    proto_blocks = proto_wide.reshape(num_blocks, block_size, D)

    def block_scores(proto_blk):
        return jnp.einsum('vbd,kd->vbk', emb_wide, proto_blk)
    weights = jnp.ones((2, SAMPLES), jnp.float32)
    scale_blocks = jnp.ones((num_blocks, 2, block_size), jnp.float32)
    for sweep in range(ITERS):

        def column_sums(proto_blk, weights=weights):
            sink_exp = jnp.exp(block_scores(proto_blk) / EPS_SINK)
            return 1.0 / lax.optimization_barrier(jnp.sum(sink_exp * weights[:, :, None], axis=1))
        scale_blocks = lax.map(column_sums, proto_blocks)

        def row_part(running, inputs):
            proto_blk, scale_blk = inputs
            sink_exp = jnp.exp(block_scores(proto_blk) / EPS_SINK)
            return (running + lax.optimization_barrier(jnp.sum(sink_exp * scale_blk[:, None, :], axis=2)), None)
        totals, ignored = lax.scan(row_part, jnp.zeros((2, SAMPLES), jnp.float32), (proto_blocks, scale_blocks))
        weights = 1.0 / totals

    def assignment(scores, scale_blk):
        return jnp.exp(scores / EPS_SINK) * scale_blk[:, None, :] * weights[:, :, None]

    def final_pass(running, inputs):
        proto_blk, scale_blk = inputs
        scores = block_scores(proto_blk)
        swapped = assignment(scores, scale_blk)[::-1]
        soft_sum = lax.optimization_barrier(jnp.sum(jnp.exp(scores / TEMPER), axis=2))
        cross_sum = lax.optimization_barrier(jnp.sum(swapped * scores, axis=2))
        mass_sum = lax.optimization_barrier(jnp.sum(swapped, axis=2))
        return ((running[0] + soft_sum, running[1] + cross_sum, running[2] + mass_sum), None)
    zeros_rows = jnp.zeros((2, SAMPLES), jnp.float32)
    sums_out, ignored = lax.scan(final_pass, (zeros_rows, zeros_rows, zeros_rows), (proto_blocks, scale_blocks))
    soft_total, cross_total, mass_total = sums_out
    loss = jnp.log(soft_total) * mass_total - cross_total / TEMPER

    def grad_pass(running, inputs):
        proto_blk, scale_blk = inputs
        scores = block_scores(proto_blk)
        swapped = assignment(scores, scale_blk)[::-1]
        softmax_p = jnp.exp(scores / TEMPER) / soft_total[:, :, None]
        slope_bf = ((softmax_p - swapped) / TEMPER).astype(jnp.bfloat16)
        slope_wide = lax.optimization_barrier(slope_bf).astype(jnp.float32)
        running = running + jnp.einsum('vbk,kd->vbd', slope_wide, proto_blk)
        proto_part = jnp.einsum('vbk,vbd->kd', slope_wide, emb_wide)
        return (running, proto_part)
    emb_grad, proto_parts = lax.scan(grad_pass, jnp.zeros((2, SAMPLES, D), jnp.float32), (proto_blocks, scale_blocks))
    proto_grad = proto_parts.reshape(PROTOS, D)
    grad_embed = project(emb_grad, unit_emb, inverse_emb).astype(jnp.bfloat16)
    grad_proto = project(proto_grad, unit_proto, inverse_proto).astype(jnp.bfloat16)
    return (grad_embed, grad_proto, loss)
```

```python
import functools
import math

import jax
import jax.numpy as jnp
from jax import lax
from jax.experimental import pallas as pl
from jax.experimental.pallas import tpu as pltpu
from jax.sharding import PartitionSpec as P

ITERS = 3


EPS_SINK = 0.05
TEMPER = 0.1
RADIX = 8
STEP = 2
LOG2E = math.log2(math.e)
VMEM = pl.BlockSpec(memory_space=pltpu.VMEM)
SMEM = pl.BlockSpec(memory_space=pltpu.SMEM)
ANY = pl.BlockSpec(memory_space=pl.ANY)
PARAMS = pltpu.CompilerParams(vmem_limit_bytes=24 << 20)
SMALL = pltpu.CompilerParams(vmem_limit_bytes=8 << 20)


def normalize_rows(values):
    as_float = values.astype(jnp.float32)
    inverse = lax.rsqrt(jnp.sum(as_float * as_float, axis=-1, keepdims=True) + 1e-06)
    return (as_float * inverse, inverse)


def project(summed, unit_rows, inverse):
    return (summed - unit_rows * jnp.sum(unit_rows * summed, axis=-1, keepdims=True)) * inverse


def groups_of(size, first, later=RADIX):
    found, stride, limit = [], 1, first
    while stride < size:
        radix = min(limit, size // stride)
        found.append((stride, radix))
        stride, limit = stride * radix, later
    return found


def swap(value, axis, size, mask):
    return lax.ppermute(value, axis, [(i, i ^ mask) for i in range(size)])


def tree_sum(parts):
    while len(parts) > 1:
        parts = [parts[i] + parts[i + 1] for i in range(0, len(parts), 2)]
    return parts[0]


def sum_all(value, axis, size):
    for stride, radix in groups_of(size, STEP, STEP):
        value = tree_sum([value] + [swap(value, axis, size, stride * j) for j in range(1, radix)])
    return value


def digit_of(axis, stride, radix):
    return (lax.axis_index(axis) // stride) % radix


def scatter_sum(value, axis, size, first):
    value = value[None]
    for stride, radix in groups_of(size, first):
        digit = digit_of(axis, stride, radix)
        value = value.reshape((radix, -1) + value.shape[2:]) if value.shape[0] == 1 else value
        parts = [lax.dynamic_index_in_dim(value, digit ^ j, 0, keepdims=False) for j in range(radix)]
        got = [parts[0]] + [swap(parts[j], axis, size, stride * j) for j in range(1, radix)]
        value = tree_sum(got)[None]
    return value[0, 0]


def own_entry(axis, size, first):
    entry, left = 0, size
    for stride, radix in groups_of(size, first):
        left //= radix
        entry = entry + digit_of(axis, stride, radix) * left
    return entry


def gather_all(value, axis, size, first):
    value = value[None]
    for stride, radix in reversed(groups_of(size, first)):
        digit = digit_of(axis, stride, radix)
        got = [value] + [swap(value, axis, size, stride * j) for j in range(1, radix)]
        whole = jnp.zeros((radix,) + value.shape, value.dtype)
        for j in range(radix):
            whole = lax.dynamic_update_index_in_dim(whole, got[j], digit ^ j, 0)
        value = whole.reshape((-1,) + value.shape[1:])
    return value


def body_large(samp, proto, embeddings, prototypes):
    per_view = embeddings.shape[1]
    width = embeddings.shape[2]
    unit_emb, inverse_emb = normalize_rows(embeddings)
    unit_proto, inverse_proto = normalize_rows(prototypes)
    emb_b = unit_emb.astype(jnp.bfloat16)
    proto_b = unit_proto.astype(jnp.bfloat16)
    scores = jnp.einsum("vbd,kd->vbk", emb_b, proto_b, preferred_element_type=jnp.float32)
    sink_exp = jnp.exp(scores / EPS_SINK)
    soft_exp = jnp.exp(scores / TEMPER)
    weights = jnp.ones((2, per_view), jnp.float32)
    proto_scale = jnp.ones((2, scores.shape[2]), jnp.float32)
    soft_total = weights
    cross_total = weights
    for sweep in range(ITERS):
        column_sums = jnp.sum(sink_exp * weights[:, :, None], axis=1)
        proto_scale = 1.0 / sum_all(column_sums, "samp", samp)
        row_sums = jnp.sum(sink_exp * proto_scale[:, None, :], axis=2)
        extras = []
        if sweep == 0:
            extras.append(jnp.sum(soft_exp, axis=2))
        if sweep == ITERS - 1:
            scaled_swap = (sink_exp * proto_scale[:, None, :])[::-1]
            extras.append(jnp.sum(scaled_swap * scores, axis=2))
        totals = sum_all(jnp.stack([row_sums] + extras), "proto", proto)
        weights = 1.0 / totals[0]
        if sweep == 0:
            soft_total = totals[1]
        if sweep == ITERS - 1:
            cross_total = totals[len(extras)]
    loss = jnp.log(soft_total) - cross_total * weights[::-1] / TEMPER
    assign = sink_exp * proto_scale[:, None, :] * weights[:, :, None]
    softmax_p = soft_exp / soft_total[:, :, None]
    slope_bf = ((softmax_p - assign[::-1]) / TEMPER).astype(jnp.bfloat16)

    emb_part = jnp.einsum("vbk,kd->vbd", slope_bf, proto_b, preferred_element_type=jnp.float32)
    rows = per_view // proto
    emb_part = emb_part.reshape(2, proto, rows, width).transpose(1, 0, 2, 3)
    emb_grad = scatter_sum(emb_part, "proto", proto, 2)
    entry = own_entry("proto", proto, 2)
    own_unit = lax.dynamic_slice_in_dim(unit_emb, entry * rows, rows, 1)
    own_inverse = lax.dynamic_slice_in_dim(inverse_emb, entry * rows, rows, 1)
    own_embed = project(emb_grad, own_unit, own_inverse).astype(jnp.bfloat16)

    proto_part = jnp.einsum("vbk,vbd->kd", slope_bf, emb_b, preferred_element_type=jnp.float32)
    lines = prototypes.shape[0] // samp
    proto_grad = scatter_sum(proto_part.reshape(samp, lines, width), "samp", samp, RADIX)
    entry = own_entry("samp", samp, RADIX)
    own_unit = lax.dynamic_slice_in_dim(unit_proto, entry * lines, lines, 0)
    own_inverse = lax.dynamic_slice_in_dim(inverse_proto, entry * lines, lines, 0)
    own_proto = project(proto_grad, own_unit, own_inverse).astype(jnp.bfloat16)

    grad_proto = gather_all(own_proto, "samp", samp, RADIX).reshape(prototypes.shape)
    grad_embed = gather_all(own_embed, "proto", proto, 2)
    grad_embed = grad_embed.transpose(1, 0, 2, 3).reshape(embeddings.shape)
    return (grad_embed, grad_proto, loss)


def dot_t(a, b):
    return lax.dot_general(a, b, (((1,), (1,)), ((), ())), preferred_element_type=jnp.float32)


def dot_n(a, b):
    return lax.dot_general(a, b, (((1,), (0,)), ((), ())), preferred_element_type=jnp.float32)


def unit_kernel(*refs):
    half = len(refs) // 2
    for raw_ref, out_ref in zip(refs[:half], refs[half:]):
        out_ref[...] = normalize_rows(raw_ref[...])[0].astype(jnp.bfloat16)


def score_kernel(tile, emb_ref, proto_ref, sink_ref, soft_ref, *column_refs):
    rows = emb_ref.shape[0] // 2
    for view in range(2):
        emb = emb_ref[view * rows:(view + 1) * rows]
        total = jnp.zeros((8, rows), jnp.float32)
        for at in range(0, proto_ref.shape[0], tile):
            soft = jnp.exp2(dot_t(proto_ref[at:at + tile], emb) * (LOG2E / TEMPER))
            sink = soft * soft
            sink_ref[view, at:at + tile] = sink
            total = total + jnp.sum(soft.reshape(-1, 8, rows), axis=0)
            for column_ref in column_refs:
                lanes = sum(sink[:, lane:lane + 128] for lane in range(0, rows, 128))
                column_ref[view:view + 1, at:at + tile] = jnp.sum(lanes.T, axis=0, keepdims=True)
        soft_ref[view:view + 1] = jnp.sum(total, axis=0, keepdims=True)


def sweep_kernel(last, tile, weight_ref, own_ref, one_ref, two_ref, three_ref, *refs):
    out_ref = refs[-1]
    blocks = (own_ref, one_ref, two_ref, three_ref)
    _, count, rows = own_ref.shape
    if last:
        cross = [jnp.zeros((8, rows), jnp.float32)] * 2
        out_ref[...] = jnp.zeros(out_ref.shape, jnp.float32)
    for view in range(2):
        weight = [jnp.broadcast_to(weight_ref[2 * at + view:2 * at + view + 1], (8, rows)) for at in range(4)]
        totals = [jnp.zeros((8, rows), jnp.float32)] * 4
        for first in range(0, count, tile):
            part = slice(first, first + tile)
            lanes = []
            for at in range(4):
                scaled = blocks[at][view, part].reshape(-1, 8, rows) * weight[at]
                scaled = scaled.reshape(tile, rows)
                lanes.append(sum(scaled[:, lane:lane + 128] for lane in range(0, rows, 128)))
            scale = 1.0 / jnp.sum(tree_sum(lanes), axis=1, keepdims=True)
            for at in range(4):
                scaled = blocks[at][view, part] * scale
                totals[at] = totals[at] + jnp.sum(scaled.reshape(-1, 8, rows), axis=0)
                if last and at == 0:
                    scaled = scaled * (jnp.log(own_ref[1 - view, part]) * EPS_SINK)
                    cross[1 - view] = cross[1 - view] + jnp.sum(scaled.reshape(-1, 8, rows), axis=0)
            if last:
                line = 10 + 2 * view + first // rows
                out_ref[line:line + 1, first % rows:first % rows + tile] = jnp.broadcast_to(scale, (tile, 128)).T[:1]
        for at in range(4):
            out_ref[2 * at + view:2 * at + view + 1] = jnp.sum(totals[at], axis=0, keepdims=True)
    if last:
        for view in range(2):
            out_ref[8 + view:9 + view] = jnp.sum(cross[view], axis=0, keepdims=True)
    else:
        for at in range(4):
            out_ref[8 + 2 * at:10 + 2 * at] = refs[at][...]


def found_kernel(mine_ref, theirs_ref, soft_ref, out_ref):
    totals = mine_ref[:10] + theirs_ref[:10]
    weights = 1.0 / totals[:8]
    soft = soft_ref[...]
    for view in range(2):
        crossed = totals[8 + view:9 + view] * weights[1 - view:2 - view]
        out_ref[view:view + 1] = jnp.log(soft[view:view + 1]) - crossed / TEMPER
    out_ref[2:10] = mine_ref[10:18]
    out_ref[10:18] = theirs_ref[10:18]
    out_ref[18:26] = weights / TEMPER
    out_ref[26:34] = 1.0 / (TEMPER * soft)


def finish(summed, raw):
    unit, inverse = normalize_rows(raw)
    return project(summed, unit, inverse).astype(jnp.bfloat16)


def column(row):
    return jnp.broadcast_to(row, (128, row.shape[1])).T


def widen(col, lanes):
    return jnp.concatenate([col] * (lanes // 128), axis=1)


def scale_row(found_ref, block, view, half):
    line = 2 + 4 * block + 2 * view + half
    return found_ref[line:line + 1]


def weight_row(found_ref, block, view):
    line = 18 + 2 * block + view
    return found_ref[line:line + 1]


def soft_row(found_ref, block, view):
    line = 26 + 2 * block + view
    return found_ref[line:line + 1]


def pipeline(steps, products_of, factors_of, place, soft_ref, slope_ref, rows):
    def slopes(step, first, last):
        slot = step % 2
        own_of, other_of = factors_of(step)
        for at in range(first, last, 16):
            part = slice(at, at + 16)
            soft = [jnp.exp2(soft_ref[(slot,) + place(view, part)] * (LOG2E / TEMPER)) for view in range(2)]
            taken = [other_of(view, part, soft[view] * soft[view]) for view in range(2)]
            for view in range(2):
                slope = own_of(view, part, soft[view]) - taken[1 - view]
                slope_ref[(slot,) + place(view, part)] = slope.astype(jnp.bfloat16)

    for step in range(-1, steps + 1):
        products = products_of(step + 1 if step + 1 < steps else None, step - 1 if step >= 1 else None)
        cuts = [rows * at // len(products) // 16 * 16 for at in range(len(products) + 1)]
        for at, product in enumerate(products):
            product()
            if 0 <= step < steps:
                slopes(step, cuts[at], cuts[at + 1])


def fetch_rows(sources, rows_ref, sem_ref):
    fetches = [pltpu.make_async_copy(source, rows_ref.at[at], sem_ref.at[at]) for at, source in enumerate(sources)]
    for fetch in fetches:
        fetch.start()
    return fetches


def proto_grad_kernel(tile, own_ref, one_ref, two_ref, three_ref, proto_ref, raw_ref, lead_raw_ref, found_ref,
                      out_ref, loss_ref, col_ref, acc_ref, work_ref, slope_ref, rows_ref, sem_ref):
    fetches = fetch_rows((raw_ref, lead_raw_ref), rows_ref, sem_ref)
    loss_ref[...] = found_ref[:2]
    blocks = (own_ref, one_ref, two_ref, three_ref)
    rows = own_ref.shape[0] // 2
    tiles = proto_ref.shape[0] // tile
    for view in range(2):
        for first in range(0, proto_ref.shape[0], rows):
            col_ref[view, first:first + rows] = column(scale_row(found_ref, 0, view, first // rows))

    def score(step, at):
        first = step % tiles * tile
        proto = proto_ref[first:first + tile]
        work_ref[step % 2, :, at:at + 256] = dot_t(proto, blocks[step // tiles][at:at + 256])

    def gradient(step):
        first = step % tiles * tile
        acc_ref[step // tiles, first:first + tile] = dot_n(slope_ref[step % 2], blocks[step // tiles][...])

    def products_of(ahead, behind):
        scores = [] if ahead is None else [functools.partial(score, ahead, at) for at in range(0, 2 * rows, 256)]
        grads = [] if behind is None else [functools.partial(gradient, behind)]
        half = len(scores) // 2
        return scores[:half] + grads + scores[half:]

    def factors_of(step):
        block = step // tiles
        soft = [jnp.broadcast_to(soft_row(found_ref, block, view), (16, rows)) for view in range(2)]
        weight = [jnp.broadcast_to(weight_row(found_ref, block, view), (16, rows)) for view in range(2)]
        base = step % tiles * tile

        def other_of(view, part, sink):
            return sink * widen(col_ref[view, base + part.start:base + part.stop], rows) * weight[view]

        return (lambda view, part, value: value * soft[view]), other_of

    def place(view, part):
        return part, slice(view * rows, (view + 1) * rows)

    pipeline(len(blocks) * tiles, products_of, factors_of, place, work_ref, slope_ref, tile)
    half = raw_ref.shape[0]
    for at in range(2):
        part = slice(at * half, (at + 1) * half)
        fetches[at].wait()
        out_ref[at] = finish(tree_sum([acc_ref[block, part] for block in range(4)]), rows_ref[at])


def emb_grad_kernel(tile, own_ref, one_ref, two_ref, three_ref, emb_ref, raw_ref, found_ref,
                    out_ref, loss_ref, col_ref, acc_ref, work_ref, slope_ref, rows_ref, sem_ref):
    fetches = fetch_rows((raw_ref.at[0], raw_ref.at[1]), rows_ref, sem_ref)
    loss_ref[...] = found_ref[:2]
    blocks = (own_ref, one_ref, two_ref, three_ref)
    rows = emb_ref.shape[0] // 2
    tiles = own_ref.shape[0] // tile
    for view in range(2):
        col_ref[view] = column(soft_row(found_ref, 0, view))
        col_ref[2 + view] = column(weight_row(found_ref, 0, view))

    def score(step, at):
        first = step % tiles * tile + at
        work_ref[step % 2, :, at:at + 256] = dot_t(emb_ref[...], blocks[step // tiles][first:first + 256])

    def gradient(step):
        block, first = step // tiles, step % tiles * tile
        grad = dot_n(slope_ref[step % 2], blocks[block][first:first + tile])
        if step % tiles:
            grad = grad + acc_ref[block]
        acc_ref[block] = grad

    def products_of(ahead, behind):
        scores = [] if ahead is None else [functools.partial(score, ahead, at) for at in range(0, tile, 256)]
        grads = [] if behind is None else [functools.partial(gradient, behind)]
        return scores[:1] + grads + scores[1:]

    def factors_of(step):
        block, half = step // tiles, step % tiles
        scale = [jnp.broadcast_to(scale_row(found_ref, block, view, half), (16, tile)) for view in range(2)]

        def own_of(view, part, value):
            return value * widen(col_ref[view, part], tile)

        def other_of(view, part, sink):
            return sink * scale[view] * widen(col_ref[2 + view, part], tile)

        return own_of, other_of

    def place(view, part):
        return (slice(view * rows + part.start, view * rows + part.stop),)

    pipeline(len(blocks) * tiles, products_of, factors_of, place, work_ref, slope_ref, rows)
    for view in range(2):
        part = slice(view * rows, (view + 1) * rows)
        total = tree_sum([acc_ref[block, part] for block in range(len(blocks))])
        fetches[view].wait()
        out_ref[view] = finish(total, rows_ref[view])


def own_part_kernel(core_ref, mine_ref, embed_ref, proto_ref, sem_ref):
    @pl.when(core_ref[0] == 0)
    def _():
        copy = pltpu.make_async_copy(mine_ref, embed_ref, sem_ref)
        copy.start()
        copy.wait()

    @pl.when(core_ref[0] == 1)
    def _():
        copy = pltpu.make_async_copy(mine_ref.at[1], proto_ref, sem_ref)
        copy.start()
        copy.wait()


def other_part_kernel(core_ref, theirs_ref, embed_in_ref, proto_in_ref, embed_ref, proto_ref, sem_ref):
    @pl.when(core_ref[0] == 0)
    def _():
        copy = pltpu.make_async_copy(theirs_ref.at[0], proto_ref, sem_ref)
        copy.start()
        copy.wait()

    @pl.when(core_ref[0] == 1)
    def _():
        copy = pltpu.make_async_copy(theirs_ref, embed_ref, sem_ref)
        copy.start()
        copy.wait()


def chip_masks(size, bits):
    return [bits << i for i in range((size // bits).bit_length() - 1)]


def chip_sum(value, axis, size, bits):
    for mask in chip_masks(size, bits):
        value = value + swap(value, axis, size, mask)
    return value


def chip_gather(value, axis, size, bits):
    value = value[None]
    for mask in chip_masks(size, bits):
        value = jnp.concatenate([value, swap(value, axis, size, mask)])
    return value


def scored(flat, proto_b, columns):
    rows, width = flat.shape
    count = proto_b.shape[0]
    shapes = [(2, count, rows // 2), (2, rows // 2)] + [(2, count)] * columns
    return pl.pallas_call(
        functools.partial(score_kernel, min(count, 256)),
        out_shape=[jax.ShapeDtypeStruct(shape, jnp.float32) for shape in shapes],
        in_specs=[VMEM] * 2,
        out_specs=[VMEM] * len(shapes),
        compiler_params=SMALL,
        cost_estimate=pl.CostEstimate(
            flops=2 * rows * count * width, bytes_accessed=2 * (rows + count) * width, transcendentals=rows * count
        ),
    )(flat, proto_b)


def swept(last, weights, sinks, softs):
    _, count, rows = sinks[0].shape
    return pl.pallas_call(
        functools.partial(sweep_kernel, last, 128),
        out_shape=jax.ShapeDtypeStruct((16, rows), jnp.float32),
        in_specs=[VMEM] * (5 + len(softs)),
        out_specs=VMEM,
        compiler_params=SMALL,
        cost_estimate=pl.CostEstimate(flops=32 * rows * count, bytes_accessed=4 * rows * count, transcendentals=0),
    )(weights, *sinks, *softs)


def after(value, first):
    return lax.optimization_barrier((value, first))


def sweeps(samp, proto, flat, own, other):
    proto_b = jnp.concatenate([other, own])
    sink, soft, sums = scored(flat, proto_b, True)
    sums = sums + swap(sums, "samp", samp, 1)
    block, sums = after(flat, sums)
    one = swap(block, "samp", samp, 1)
    sums = sums + swap(sums, "samp", samp, 2)
    block, sums = after(flat, sums)
    two = swap(block, "samp", samp, 2)
    sums = jnp.sum(sink * (1.0 / sums)[:, :, None], axis=1)
    sums = sums + swap(sums, "proto", proto, 2)
    one, sums = after(one, sums)
    three = swap(one, "samp", samp, 2)
    weights = 1.0 / (sums + swap(sums, "proto", proto, 4))

    sinks, softs = [sink], [soft]
    for block in (one, two, three):
        sink, soft = scored(block, proto_b, False)
        sinks.append(sink)
        softs.append(soft)
    for mask in chip_masks(samp, 1):
        weights = jnp.concatenate([weights, swap(weights, "samp", samp, mask)])
    totals = chip_sum(swept(False, weights, sinks, softs), "proto", proto, 2)
    soft_total = totals[8:]

    totals = swept(True, 1.0 / totals[:8], sinks, [])
    got = swap(totals, "proto", proto, 2)
    totals = jnp.concatenate([totals[:10] + got[:10], totals[10:14], got[10:14]])
    found = pl.pallas_call(
        found_kernel,
        out_shape=jax.ShapeDtypeStruct((34, flat.shape[0] // 2), jnp.float32),
        in_specs=[VMEM] * 3,
        out_specs=VMEM,
        compiler_params=SMALL,
    )(totals, swap(totals, "proto", proto, 4), soft_total)
    return found, one, two, three


def gathers(proto, flat, own, other):
    proto_b = jnp.concatenate([own, other])

    def middle(value):
        return lax.ppermute(value, "proto", [(2, 4), (4, 2)])

    one = swap(proto_b, "proto", proto, 2)
    near = middle(proto_b)
    far = middle(one)
    outer_near = swap(near, "proto", proto, 2)
    outer_far = swap(far, "proto", proto, 2)
    chip = lax.axis_index("proto") // 2
    inner = (chip == 1) | (chip == 2)
    two = jnp.where(inner, far, outer_near)
    three = jnp.where(inner, near, outer_far)
    return jnp.zeros((34, flat.shape[0] // 2), jnp.float32), one, two, three


def unit_rows(*raws):
    return pl.pallas_call(
        unit_kernel,
        out_shape=[jax.ShapeDtypeStruct(raw.shape, jnp.bfloat16) for raw in raws],
        in_specs=[VMEM] * len(raws),
        out_specs=[VMEM] * len(raws),
        compiler_params=SMALL,
    )(*raws)


def body(samp, proto, embeddings, prototypes):
    _, per_view, width = embeddings.shape
    count = prototypes.shape[0]
    core = lax.axis_index("proto") % 2
    lead = core == 1
    raw_other = swap(prototypes, "proto", proto, 1)
    flat, own = unit_rows(embeddings.reshape(2 * per_view, width), prototypes)
    other, = unit_rows(raw_other)
    found, *gathered = lax.cond(
        lead, functools.partial(sweeps, samp, proto), functools.partial(gathers, proto), flat, own, other
    )
    taken = swap(found, "proto", proto, 1)
    tile = min(2 * count, 512)

    def grads(kernel, operands, raws, columns, rows, lanes):
        return pl.pallas_call(
            functools.partial(kernel, rows if kernel is proto_grad_kernel else lanes),
            out_shape=(
                jax.ShapeDtypeStruct((2, per_view, width), jnp.bfloat16),
                jax.ShapeDtypeStruct((2, per_view), jnp.float32),
            ),
            in_specs=[VMEM] * len(operands) + [ANY] * len(raws) + [VMEM],
            out_specs=(VMEM,) * 2,
            scratch_shapes=[
                pltpu.VMEM(columns, jnp.float32),
                pltpu.VMEM((4, 2 * count, width), jnp.float32),
                pltpu.VMEM((2, rows, lanes), jnp.float32),
                pltpu.VMEM((2, rows, lanes), jnp.bfloat16),
                pltpu.VMEM((2, per_view, width), jnp.bfloat16),
                pltpu.SemaphoreType.DMA((2,)),
            ],
            compiler_params=PARAMS,
        )(*operands, *raws, found if kernel is proto_grad_kernel else taken)[::-1]

    def proto_grads(flat, own, other, *gathered):
        proto_b = jnp.concatenate([other, own])
        operands = (flat, *gathered, proto_b)
        return grads(proto_grad_kernel, operands, (raw_other, prototypes), (2, 2 * count, 128), 2 * count, 2 * per_view)

    def emb_grads(flat, own, other, *gathered):
        proto_b = jnp.concatenate([own, other])
        operands = (proto_b, *gathered, flat)
        return grads(emb_grad_kernel, operands, (embeddings,), (4, per_view, 128), 2 * per_view, tile)

    loss, mine = lax.cond(lead, proto_grads, emb_grads, flat, own, other, *gathered)
    theirs = swap(mine, "proto", proto, 1)
    outputs = (
        jax.ShapeDtypeStruct(embeddings.shape, jnp.bfloat16),
        jax.ShapeDtypeStruct(prototypes.shape, jnp.bfloat16),
    )
    half_done = pl.pallas_call(
        own_part_kernel,
        out_shape=outputs,
        in_specs=[SMEM, ANY],
        out_specs=(ANY, ANY),
        scratch_shapes=[pltpu.SemaphoreType.DMA],
        compiler_params=SMALL,
    )(core.reshape(1), mine)
    grad_embed, grad_proto = pl.pallas_call(
        other_part_kernel,
        out_shape=outputs,
        in_specs=[SMEM, ANY, ANY, ANY],
        out_specs=(ANY, ANY),
        scratch_shapes=[pltpu.SemaphoreType.DMA],
        input_output_aliases={2: 0, 3: 1},
        compiler_params=SMALL,
    )(core.reshape(1), theirs, *half_done)
    return grad_embed, grad_proto, loss


def solution(mesh):
    samp, proto = mesh.shape["samp"], mesh.shape["proto"]

    def run(embeddings, prototypes):
        paired = samp == 4 and proto == 8 and prototypes.shape[0] == embeddings.shape[1] == 512
        return (body if paired else body_large)(samp, proto, embeddings, prototypes)

    return jax.shard_map(
        run,
        mesh=mesh,
        in_specs=(P(None, "samp", None), P("proto", None)),
        out_specs=(P(None, "samp", None), P("proto", None), P(None, "samp")),
        check_vma=False,
    )
```

```python
import functools
import math

import jax
import jax.numpy as jnp
from jax import lax
from jax.experimental import pallas as pl
from jax.experimental.pallas import tpu as pltpu
from jax.sharding import PartitionSpec as P

ITERS = 3


EPS_SINK = 0.05
TEMPER = 0.1
RADIX = 8
STEP = 2
LOG2E = math.log2(math.e)
VMEM = pl.BlockSpec(memory_space=pltpu.VMEM)
SMEM = pl.BlockSpec(memory_space=pltpu.SMEM)
ANY = pl.BlockSpec(memory_space=pl.ANY)
HBM = pl.BlockSpec(memory_space=pltpu.HBM)
PARAMS = pltpu.CompilerParams(vmem_limit_bytes=24 << 20)
SMALL = pltpu.CompilerParams(vmem_limit_bytes=8 << 20)


def normalize_rows(values):
    as_float = values.astype(jnp.float32)
    inverse = lax.rsqrt(jnp.sum(as_float * as_float, axis=-1, keepdims=True) + 1e-06)
    return (as_float * inverse, inverse)


def project(summed, unit_rows, inverse):
    return (summed - unit_rows * jnp.sum(unit_rows * summed, axis=-1, keepdims=True)) * inverse


def groups_of(size, first, later=RADIX):
    found, stride, limit = [], 1, first
    while stride < size:
        radix = min(limit, size // stride)
        found.append((stride, radix))
        stride, limit = stride * radix, later
    return found


def swap(value, axis, size, mask):
    return lax.ppermute(value, axis, [(i, i ^ mask) for i in range(size)])


def tree_sum(parts):
    while len(parts) > 1:
        parts = [parts[i] + parts[i + 1] for i in range(0, len(parts), 2)]
    return parts[0]


def sum_all(value, axis, size):
    for stride, radix in groups_of(size, STEP, STEP):
        value = tree_sum([value] + [swap(value, axis, size, stride * j) for j in range(1, radix)])
    return value


def digit_of(axis, stride, radix):
    return (lax.axis_index(axis) // stride) % radix


def scatter_sum(value, axis, size, first):
    value = value[None]
    for stride, radix in groups_of(size, first):
        digit = digit_of(axis, stride, radix)
        value = value.reshape((radix, -1) + value.shape[2:]) if value.shape[0] == 1 else value
        parts = [lax.dynamic_index_in_dim(value, digit ^ j, 0, keepdims=False) for j in range(radix)]
        got = [parts[0]] + [swap(parts[j], axis, size, stride * j) for j in range(1, radix)]
        value = tree_sum(got)[None]
    return value[0, 0]


def own_entry(axis, size, first):
    entry, left = 0, size
    for stride, radix in groups_of(size, first):
        left //= radix
        entry = entry + digit_of(axis, stride, radix) * left
    return entry


def gather_all(value, axis, size, first):
    value = value[None]
    for stride, radix in reversed(groups_of(size, first)):
        digit = digit_of(axis, stride, radix)
        got = [value] + [swap(value, axis, size, stride * j) for j in range(1, radix)]
        whole = jnp.zeros((radix,) + value.shape, value.dtype)
        for j in range(radix):
            whole = lax.dynamic_update_index_in_dim(whole, got[j], digit ^ j, 0)
        value = whole.reshape((-1,) + value.shape[1:])
    return value


def body_large(samp, proto, embeddings, prototypes):
    per_view = embeddings.shape[1]
    width = embeddings.shape[2]
    unit_emb, inverse_emb = normalize_rows(embeddings)
    unit_proto, inverse_proto = normalize_rows(prototypes)
    emb_b = unit_emb.astype(jnp.bfloat16)
    proto_b = unit_proto.astype(jnp.bfloat16)
    scores = jnp.einsum("vbd,kd->vbk", emb_b, proto_b, preferred_element_type=jnp.float32)
    sink_exp = jnp.exp(scores / EPS_SINK)
    soft_exp = jnp.exp(scores / TEMPER)
    weights = jnp.ones((2, per_view), jnp.float32)
    proto_scale = jnp.ones((2, scores.shape[2]), jnp.float32)
    soft_total = weights
    cross_total = weights
    for sweep in range(ITERS):
        column_sums = jnp.sum(sink_exp * weights[:, :, None], axis=1)
        proto_scale = 1.0 / sum_all(column_sums, "samp", samp)
        row_sums = jnp.sum(sink_exp * proto_scale[:, None, :], axis=2)
        extras = []
        if sweep == 0:
            extras.append(jnp.sum(soft_exp, axis=2))
        if sweep == ITERS - 1:
            scaled_swap = (sink_exp * proto_scale[:, None, :])[::-1]
            extras.append(jnp.sum(scaled_swap * scores, axis=2))
        totals = sum_all(jnp.stack([row_sums] + extras), "proto", proto)
        weights = 1.0 / totals[0]
        if sweep == 0:
            soft_total = totals[1]
        if sweep == ITERS - 1:
            cross_total = totals[len(extras)]
    loss = jnp.log(soft_total) - cross_total * weights[::-1] / TEMPER
    assign = sink_exp * proto_scale[:, None, :] * weights[:, :, None]
    softmax_p = soft_exp / soft_total[:, :, None]
    slope_bf = ((softmax_p - assign[::-1]) / TEMPER).astype(jnp.bfloat16)

    emb_part = jnp.einsum("vbk,kd->vbd", slope_bf, proto_b, preferred_element_type=jnp.float32)
    rows = per_view // proto
    emb_part = emb_part.reshape(2, proto, rows, width).transpose(1, 0, 2, 3)
    emb_grad = scatter_sum(emb_part, "proto", proto, 2)
    entry = own_entry("proto", proto, 2)
    own_unit = lax.dynamic_slice_in_dim(unit_emb, entry * rows, rows, 1)
    own_inverse = lax.dynamic_slice_in_dim(inverse_emb, entry * rows, rows, 1)
    own_embed = project(emb_grad, own_unit, own_inverse).astype(jnp.bfloat16)

    proto_part = jnp.einsum("vbk,vbd->kd", slope_bf, emb_b, preferred_element_type=jnp.float32)
    lines = prototypes.shape[0] // samp
    proto_grad = scatter_sum(proto_part.reshape(samp, lines, width), "samp", samp, RADIX)
    entry = own_entry("samp", samp, RADIX)
    own_unit = lax.dynamic_slice_in_dim(unit_proto, entry * lines, lines, 0)
    own_inverse = lax.dynamic_slice_in_dim(inverse_proto, entry * lines, lines, 0)
    own_proto = project(proto_grad, own_unit, own_inverse).astype(jnp.bfloat16)

    grad_proto = gather_all(own_proto, "samp", samp, RADIX).reshape(prototypes.shape)
    grad_embed = gather_all(own_embed, "proto", proto, 2)
    grad_embed = grad_embed.transpose(1, 0, 2, 3).reshape(embeddings.shape)
    return (grad_embed, grad_proto, loss)


def dot_t(a, b):
    return lax.dot_general(a, b, (((1,), (1,)), ((), ())), preferred_element_type=jnp.float32)


def dot_n(a, b):
    return lax.dot_general(a, b, (((1,), (0,)), ((), ())), preferred_element_type=jnp.float32)


def unit_kernel(*refs):
    half = len(refs) // 2
    for raw_ref, out_ref in zip(refs[:half], refs[half:]):
        out_ref[...] = normalize_rows(raw_ref[...])[0].astype(jnp.bfloat16)


def score_kernel(tile, emb_ref, proto_ref, sink_ref, *sum_refs):
    rows = emb_ref.shape[0] // 2
    for view in range(2):
        emb = emb_ref[view * rows:(view + 1) * rows]
        total = jnp.zeros((8, rows), jnp.float32)
        for at in range(0, proto_ref.shape[0], tile):
            soft = jnp.exp2(dot_t(proto_ref[at:at + tile], emb) * (LOG2E / TEMPER))
            sink = soft * soft
            sink_ref[view, at:at + tile] = sink
            if sum_refs:
                total = total + jnp.sum(soft.reshape(-1, 8, rows), axis=0)
                lanes = sum(sink[:, lane:lane + 128] for lane in range(0, rows, 128))
                sum_refs[1][view:view + 1, at:at + tile] = jnp.sum(lanes.T, axis=0, keepdims=True)
        if sum_refs:
            sum_refs[0][view:view + 1] = jnp.sum(total, axis=0, keepdims=True)


def lane_sums(weight_ref, block, view, at, part):
    values = block[view, part]
    tile, rows = values.shape
    weight = jnp.broadcast_to(weight_ref[2 * at + view:2 * at + view + 1], (8, rows))
    scaled = (values.reshape(-1, 8, rows) * weight).reshape(tile, rows)
    return sum(scaled[:, lane:lane + 128] for lane in range(0, rows, 128))


def column_kernel(tile, weight_ref, own_ref, one_ref, two_ref, out_ref):
    for view in range(2):
        for first in range(0, own_ref.shape[1], tile):
            part = slice(first, first + tile)
            own, one, two = (lane_sums(weight_ref, block, view, at, part) for at, block in enumerate((own_ref, one_ref, two_ref)))
            out_ref[0, view, part] = own + one
            out_ref[1, view, part] = two


def sweep_kernel(last, tile, weight_ref, own_ref, one_ref, two_ref, three_ref, *refs):
    out_ref = refs[-1]
    blocks = (own_ref, one_ref, two_ref, three_ref)
    _, count, rows = own_ref.shape
    if last:
        cross = [jnp.zeros((8, rows), jnp.float32)] * 2
        out_ref[...] = jnp.zeros(out_ref.shape, jnp.float32)
    for view in range(2):
        totals = [jnp.zeros((8, rows), jnp.float32)] * 4
        for first in range(0, count, tile):
            part = slice(first, first + tile)
            if last:
                lanes = [lane_sums(weight_ref, blocks[at], view, at, part) for at in range(4)]
            else:
                lanes = [refs[0][0, view, part], refs[0][1, view, part] + lane_sums(weight_ref, three_ref, view, 3, part)]
            scale = 1.0 / jnp.sum(tree_sum(lanes), axis=1, keepdims=True)
            for at in range(4):
                scaled = blocks[at][view, part] * scale
                totals[at] = totals[at] + jnp.sum(scaled.reshape(-1, 8, rows), axis=0)
                if last and at == 0:
                    scaled = scaled * (jnp.log(own_ref[1 - view, part]) * EPS_SINK)
                    cross[1 - view] = cross[1 - view] + jnp.sum(scaled.reshape(-1, 8, rows), axis=0)
            if last:
                line = 10 + 2 * view + first // rows
                out_ref[line:line + 1, first % rows:first % rows + tile] = jnp.broadcast_to(scale, (tile, 128)).T[:1]
        for at in range(4):
            out_ref[2 * at + view:2 * at + view + 1] = jnp.sum(totals[at], axis=0, keepdims=True)
    if last:
        for view in range(2):
            out_ref[8 + view:9 + view] = jnp.sum(cross[view], axis=0, keepdims=True)


def found_kernel(mine_ref, theirs_ref, soft_ref, out_ref):
    totals = mine_ref[:10] + theirs_ref[:10]
    weights = 1.0 / totals[:8]
    soft = soft_ref[...]
    for view in range(2):
        crossed = totals[8 + view:9 + view] * weights[1 - view:2 - view]
        out_ref[view:view + 1] = jnp.log(soft[view:view + 1]) - crossed / TEMPER
    out_ref[2:10] = mine_ref[10:18]
    out_ref[10:18] = theirs_ref[10:18]
    out_ref[18:26] = weights / TEMPER
    out_ref[26:34] = 1.0 / (TEMPER * soft)


def finish(summed, raw):
    unit, inverse = normalize_rows(raw)
    return project(summed, unit, inverse).astype(jnp.bfloat16)


def column(row):
    return jnp.broadcast_to(row, (128, row.shape[1])).T


def widen(col, lanes):
    return jnp.concatenate([col] * (lanes // 128), axis=1)


def scale_row(found_ref, block, view, half):
    line = 2 + 4 * block + 2 * view + half
    return found_ref[line:line + 1]


def weight_row(found_ref, block, view):
    line = 18 + 2 * block + view
    return found_ref[line:line + 1]


def soft_row(found_ref, block, view):
    line = 26 + 2 * block + view
    return found_ref[line:line + 1]


def pipeline(steps, products_of, factors_of, place, soft_ref, slope_ref, rows):
    def slopes(step, first, last):
        slot = step % 2
        own_of, other_of = factors_of(step)
        for at in range(first, last, 16):
            part = slice(at, at + 16)
            soft = [jnp.exp2(soft_ref[(slot,) + place(view, part)] * (LOG2E / TEMPER)) for view in range(2)]
            taken = [other_of(view, part, soft[view] * soft[view]) for view in range(2)]
            for view in range(2):
                slope = own_of(view, part, soft[view]) - taken[1 - view]
                slope_ref[(slot,) + place(view, part)] = slope.astype(jnp.bfloat16)

    for step in range(-1, steps + 1):
        products = products_of(step + 1 if step + 1 < steps else None, step - 1 if step >= 1 else None)
        cuts = [rows * at // len(products) // 16 * 16 for at in range(len(products) + 1)]
        for at, product in enumerate(products):
            product()
            if 0 <= step < steps:
                slopes(step, cuts[at], cuts[at + 1])


def fetch_rows(sources, rows_ref, sem_ref):
    fetches = [pltpu.make_async_copy(source, rows_ref.at[at], sem_ref.at[at]) for at, source in enumerate(sources)]
    for fetch in fetches:
        fetch.start()
    return fetches


def proto_grad_kernel(tile, own_ref, one_ref, two_ref, three_ref, proto_ref, raw_ref, lead_raw_ref, found_ref,
                      out_ref, loss_ref, col_ref, acc_ref, work_ref, slope_ref, rows_ref, sem_ref):
    fetches = fetch_rows((raw_ref, lead_raw_ref), rows_ref, sem_ref)
    loss_ref[...] = found_ref[:2]
    blocks = (own_ref, one_ref, two_ref, three_ref)
    rows = own_ref.shape[0] // 2
    halves = rows // tile
    for view in range(2):
        for first in range(0, proto_ref.shape[0], rows):
            col_ref[view, first:first + rows] = column(scale_row(found_ref, 0, view, first // rows))

    def emb(step, view):
        first = view * rows + step % halves * tile
        return blocks[step // halves][first:first + tile]

    def score(step, view):
        work_ref[step % 2, :, view * tile:(view + 1) * tile] = dot_t(proto_ref[...], emb(step, view))

    def gradient(step):
        grad = dot_n(slope_ref[step % 2], jnp.concatenate([emb(step, 0), emb(step, 1)]))
        if step % halves:
            grad = grad + acc_ref[step // halves]
        acc_ref[step // halves] = grad

    def products_of(ahead, behind):
        scores = [] if ahead is None else [functools.partial(score, ahead, view) for view in range(2)]
        grads = [] if behind is None else [functools.partial(gradient, behind)]
        return scores[:1] + grads + scores[1:]

    def factors_of(step):
        block, first = step // halves, step % halves * tile
        part = slice(first, first + tile)
        soft = [jnp.broadcast_to(soft_row(found_ref, block, view)[:, part], (16, tile)) for view in range(2)]
        weight = [jnp.broadcast_to(weight_row(found_ref, block, view)[:, part], (16, tile)) for view in range(2)]

        def other_of(view, part, sink):
            return sink * widen(col_ref[view, part], tile) * weight[view]

        return (lambda view, part, value: value * soft[view]), other_of

    def place(view, part):
        return part, slice(view * tile, (view + 1) * tile)

    pipeline(len(blocks) * halves, products_of, factors_of, place, work_ref, slope_ref, proto_ref.shape[0])
    half = raw_ref.shape[0]
    for at in range(2):
        part = slice(at * half, (at + 1) * half)
        fetches[at].wait()
        out_ref[at] = finish(tree_sum([acc_ref[block, part] for block in range(4)]), rows_ref[at])


def emb_grad_kernel(tile, own_ref, one_ref, two_ref, three_ref, emb_ref, raw_ref, found_ref,
                    out_ref, loss_ref, col_ref, acc_ref, work_ref, slope_ref, rows_ref, sem_ref):
    fetches = fetch_rows((raw_ref.at[0], raw_ref.at[1]), rows_ref, sem_ref)
    loss_ref[...] = found_ref[:2]
    blocks = (own_ref, one_ref, two_ref, three_ref)
    rows = emb_ref.shape[0] // 2
    tiles = own_ref.shape[0] // tile
    for view in range(2):
        col_ref[view] = column(soft_row(found_ref, 0, view))
        col_ref[2 + view] = column(weight_row(found_ref, 0, view))

    def score(step, at):
        first = step % tiles * tile + at
        work_ref[step % 2, :, at:at + 256] = dot_t(emb_ref[...], blocks[step // tiles][first:first + 256])

    def gradient(step):
        block, first = step // tiles, step % tiles * tile
        grad = dot_n(slope_ref[step % 2], blocks[block][first:first + tile])
        if step % tiles:
            grad = grad + acc_ref[block]
        acc_ref[block] = grad

    def products_of(ahead, behind):
        scores = [] if ahead is None else [functools.partial(score, ahead, at) for at in range(0, tile, 256)]
        grads = [] if behind is None else [functools.partial(gradient, behind)]
        return scores[:1] + grads + scores[1:]

    def factors_of(step):
        block, half = step // tiles, step % tiles
        scale = [jnp.broadcast_to(scale_row(found_ref, block, view, half), (16, tile)) for view in range(2)]

        def own_of(view, part, value):
            return value * widen(col_ref[view, part], tile)

        def other_of(view, part, sink):
            return sink * scale[view] * widen(col_ref[2 + view, part], tile)

        return own_of, other_of

    def place(view, part):
        return (slice(view * rows + part.start, view * rows + part.stop),)

    pipeline(len(blocks) * tiles, products_of, factors_of, place, work_ref, slope_ref, rows)
    for view in range(2):
        part = slice(view * rows, (view + 1) * rows)
        total = tree_sum([acc_ref[block, part] for block in range(len(blocks))])
        fetches[view].wait()
        out_ref[view] = finish(total, rows_ref[view])


def own_part_kernel(core_ref, mine_ref, embed_ref, proto_ref, sem_ref):
    @pl.when(core_ref[0] == 0)
    def _():
        copy = pltpu.make_async_copy(mine_ref, embed_ref, sem_ref)
        copy.start()
        copy.wait()

    @pl.when(core_ref[0] == 1)
    def _():
        copy = pltpu.make_async_copy(mine_ref.at[1], proto_ref, sem_ref)
        copy.start()
        copy.wait()


def other_part_kernel(core_ref, theirs_ref, embed_in_ref, proto_in_ref, embed_ref, proto_ref, sem_ref):
    @pl.when(core_ref[0] == 0)
    def _():
        copy = pltpu.make_async_copy(theirs_ref.at[0], proto_ref, sem_ref)
        copy.start()
        copy.wait()

    @pl.when(core_ref[0] == 1)
    def _():
        copy = pltpu.make_async_copy(theirs_ref, embed_ref, sem_ref)
        copy.start()
        copy.wait()


def chip_masks(size, bits):
    return [bits << i for i in range((size // bits).bit_length() - 1)]


def chip_sum(value, axis, size, bits):
    for mask in chip_masks(size, bits):
        value = value + swap(value, axis, size, mask)
    return value


def chip_gather(value, axis, size, bits):
    value = value[None]
    for mask in chip_masks(size, bits):
        value = jnp.concatenate([value, swap(value, axis, size, mask)])
    return value


def scored(flat, proto_b, sums):
    rows, width = flat.shape
    count = proto_b.shape[0]
    shapes = [(2, count, rows // 2)] + [(2, rows // 2), (2, count)] * sums
    return pl.pallas_call(
        functools.partial(score_kernel, min(count, 256)),
        out_shape=[jax.ShapeDtypeStruct(shape, jnp.float32) for shape in shapes],
        in_specs=[VMEM] * 2,
        out_specs=[VMEM] * len(shapes),
        compiler_params=SMALL,
        cost_estimate=pl.CostEstimate(
            flops=2 * rows * count * width, bytes_accessed=2 * (rows + count) * width, transcendentals=rows * count
        ),
    )(flat, proto_b)


def swept(weights, sinks, *sums):
    _, count, rows = sinks[0].shape
    return pl.pallas_call(
        functools.partial(sweep_kernel, not sums, 128),
        out_shape=jax.ShapeDtypeStruct((8 if sums else 16, rows), jnp.float32),
        in_specs=[VMEM] * (5 + len(sums)),
        out_specs=VMEM,
        compiler_params=SMALL,
        cost_estimate=pl.CostEstimate(flops=32 * rows * count, bytes_accessed=4 * rows * count, transcendentals=0),
    )(weights, *sinks, *sums)


def first_sums(weights, sinks):
    _, count, rows = sinks[0].shape
    return pl.pallas_call(
        functools.partial(column_kernel, 128),
        out_shape=jax.ShapeDtypeStruct((2, 2, count, 128), jnp.float32),
        in_specs=[VMEM] * 4,
        out_specs=VMEM,
        compiler_params=SMALL,
        cost_estimate=pl.CostEstimate(flops=12 * rows * count, bytes_accessed=4 * rows * count, transcendentals=0),
    )(weights, *sinks[:3])


def after(value, first):
    return lax.optimization_barrier((value, first))


def sweeps(samp, proto, flat, own, other):
    proto_b = jnp.concatenate([other, own])
    sink, soft, sums = scored(flat, proto_b, True)
    sums = sums + swap(sums, "samp", samp, 1)
    block, sums = after(flat, sums)
    one = swap(block, "samp", samp, 1)
    two = swap(block, "samp", samp, 2)
    sums = sums + swap(sums, "samp", samp, 2)
    sums = jnp.concatenate([jnp.sum(sink * (1.0 / sums)[:, :, None], axis=1), soft])
    sums = sums + swap(sums, "proto", proto, 2)
    sums = sums + swap(sums, "proto", proto, 4)
    one, sums = after(one, sums)
    three = swap(one, "samp", samp, 2)

    sinks = [sink] + [scored(block, proto_b, False)[0] for block in (one, two, three)]
    both = jnp.concatenate([sums, swap(sums, "samp", samp, 2)])
    sums = jnp.concatenate([both, swap(both, "samp", samp, 1)])
    weights = 1.0 / jnp.concatenate([sums[at:at + 2] for at in (0, 8, 4, 12)])
    soft_total = jnp.concatenate([sums[at:at + 2] for at in (2, 10, 6, 14)])
    totals = chip_sum(swept(weights, sinks, first_sums(weights, sinks)), "proto", proto, 2)
    totals = swept(1.0 / totals, sinks)
    got = swap(totals, "proto", proto, 2)
    totals = jnp.concatenate([totals[:10] + got[:10], totals[10:14], got[10:14]])
    found = pl.pallas_call(
        found_kernel,
        out_shape=jax.ShapeDtypeStruct((34, flat.shape[0] // 2), jnp.float32),
        in_specs=[VMEM] * 3,
        out_specs=VMEM,
        compiler_params=SMALL,
    )(totals, swap(totals, "proto", proto, 4), soft_total)
    return found, one, two, three


def gathers(proto, flat, own, other):
    proto_b = jnp.concatenate([own, other])

    def middle(value):
        return lax.ppermute(value, "proto", [(2, 4), (4, 2)])

    one = swap(proto_b, "proto", proto, 2)
    near = middle(proto_b)
    far = middle(one)
    outer_near = swap(near, "proto", proto, 2)
    outer_far = swap(far, "proto", proto, 2)
    chip = lax.axis_index("proto") // 2
    inner = (chip == 1) | (chip == 2)
    two = jnp.where(inner, far, outer_near)
    three = jnp.where(inner, near, outer_far)
    return jnp.zeros((34, flat.shape[0] // 2), jnp.float32), one, two, three


def unit_rows(*raws):
    return pl.pallas_call(
        unit_kernel,
        out_shape=[jax.ShapeDtypeStruct(raw.shape, jnp.bfloat16) for raw in raws],
        in_specs=[VMEM] * len(raws),
        out_specs=[VMEM] * len(raws),
        compiler_params=SMALL,
    )(*raws)


def body(samp, proto, embeddings, prototypes):
    _, per_view, width = embeddings.shape
    count = prototypes.shape[0]
    core = lax.axis_index("proto") % 2
    lead = core == 1
    raw_other = swap(prototypes, "proto", proto, 1)
    flat, own = unit_rows(embeddings.reshape(2 * per_view, width), prototypes)
    other, = unit_rows(raw_other)
    raw_other = swap(after(prototypes, own)[0], "proto", proto, 1)
    found, *gathered = lax.cond(
        lead, functools.partial(sweeps, samp, proto), functools.partial(gathers, proto), flat, own, other
    )
    taken = swap(found, "proto", proto, 1)
    tile = min(2 * count, 512)

    def grads(kernel, operands, raws, columns, rows, lanes):
        return pl.pallas_call(
            functools.partial(kernel, lanes // 2 if kernel is proto_grad_kernel else lanes),
            out_shape=(
                jax.ShapeDtypeStruct((2, per_view, width), jnp.bfloat16),
                jax.ShapeDtypeStruct((2, per_view), jnp.float32),
            ),
            in_specs=[VMEM] * len(operands) + [HBM] * len(raws) + [VMEM],
            out_specs=(VMEM,) * 2,
            scratch_shapes=[
                pltpu.VMEM(columns, jnp.float32),
                pltpu.VMEM((4, 2 * count, width), jnp.float32),
                pltpu.VMEM((2, rows, lanes), jnp.float32),
                pltpu.VMEM((2, rows, lanes), jnp.bfloat16),
                pltpu.VMEM((2, per_view, width), jnp.bfloat16),
                pltpu.SemaphoreType.DMA((2,)),
            ],
            compiler_params=PARAMS,
        )(*operands, *raws, found if kernel is proto_grad_kernel else taken)[::-1]

    def proto_grads(flat, own, other, *gathered):
        proto_b = jnp.concatenate([other, own])
        operands = (flat, *gathered, proto_b)
        return grads(proto_grad_kernel, operands, (raw_other, prototypes), (2, 2 * count, 128), 2 * count, per_view)

    def emb_grads(flat, own, other, *gathered):
        proto_b = jnp.concatenate([own, other])
        operands = (proto_b, *gathered, flat)
        return grads(emb_grad_kernel, operands, (embeddings,), (4, per_view, 128), 2 * per_view, tile)

    loss, mine = lax.cond(lead, proto_grads, emb_grads, flat, own, other, *gathered)
    theirs = swap(mine, "proto", proto, 1)
    outputs = (
        jax.ShapeDtypeStruct(embeddings.shape, jnp.bfloat16),
        jax.ShapeDtypeStruct(prototypes.shape, jnp.bfloat16),
    )
    half_done = pl.pallas_call(
        own_part_kernel,
        out_shape=outputs,
        in_specs=[SMEM, ANY],
        out_specs=(ANY, ANY),
        scratch_shapes=[pltpu.SemaphoreType.DMA],
        compiler_params=SMALL,
    )(core.reshape(1), mine)
    grad_embed, grad_proto = pl.pallas_call(
        other_part_kernel,
        out_shape=outputs,
        in_specs=[SMEM, ANY, ANY, ANY],
        out_specs=(ANY, ANY),
        scratch_shapes=[pltpu.SemaphoreType.DMA],
        input_output_aliases={2: 0, 3: 1},
        compiler_params=SMALL,
    )(core.reshape(1), theirs, *half_done)
    return grad_embed, grad_proto, loss


def solution(mesh):
    samp, proto = mesh.shape["samp"], mesh.shape["proto"]

    def run(embeddings, prototypes):
        paired = samp == 4 and proto == 8 and prototypes.shape[0] == embeddings.shape[1] == 512
        return (body if paired else body_large)(samp, proto, embeddings, prototypes)

    return jax.shard_map(
        run,
        mesh=mesh,
        in_specs=(P(None, "samp", None), P("proto", None)),
        out_specs=(P(None, "samp", None), P("proto", None), P(None, "samp")),
        check_vma=False,
    )
```

```python
import functools
import math

import jax
import jax.numpy as jnp
from jax import lax
from jax.experimental import pallas as pl
from jax.experimental.pallas import tpu as pltpu
from jax.sharding import PartitionSpec as P

ITERS = 3


EPS_SINK = 0.05
TEMPER = 0.1
RADIX = 8
STEP = 2
LOG2E = math.log2(math.e)
VMEM = pl.BlockSpec(memory_space=pltpu.VMEM)
SMEM = pl.BlockSpec(memory_space=pltpu.SMEM)
ANY = pl.BlockSpec(memory_space=pl.ANY)
HBM = pl.BlockSpec(memory_space=pltpu.HBM)
PARAMS = pltpu.CompilerParams(vmem_limit_bytes=24 << 20)
SMALL = pltpu.CompilerParams(vmem_limit_bytes=8 << 20)


def normalize_rows(values):
    as_float = values.astype(jnp.float32)
    inverse = lax.rsqrt(jnp.sum(as_float * as_float, axis=-1, keepdims=True) + 1e-06)
    return (as_float * inverse, inverse)


def project(summed, unit_rows, inverse):
    return (summed - unit_rows * jnp.sum(unit_rows * summed, axis=-1, keepdims=True)) * inverse


def groups_of(size, first, later=RADIX):
    found, stride, limit = [], 1, first
    while stride < size:
        radix = min(limit, size // stride)
        found.append((stride, radix))
        stride, limit = stride * radix, later
    return found


def swap(value, axis, size, mask):
    return lax.ppermute(value, axis, [(i, i ^ mask) for i in range(size)])


def tree_sum(parts):
    while len(parts) > 1:
        parts = [parts[i] + parts[i + 1] for i in range(0, len(parts), 2)]
    return parts[0]


def sum_all(value, axis, size):
    for stride, radix in groups_of(size, STEP, STEP):
        value = tree_sum([value] + [swap(value, axis, size, stride * j) for j in range(1, radix)])
    return value


def digit_of(axis, stride, radix):
    return (lax.axis_index(axis) // stride) % radix


def scatter_sum(value, axis, size, first):
    value = value[None]
    for stride, radix in groups_of(size, first):
        digit = digit_of(axis, stride, radix)
        value = value.reshape((radix, -1) + value.shape[2:]) if value.shape[0] == 1 else value
        parts = [lax.dynamic_index_in_dim(value, digit ^ j, 0, keepdims=False) for j in range(radix)]
        got = [parts[0]] + [swap(parts[j], axis, size, stride * j) for j in range(1, radix)]
        value = tree_sum(got)[None]
    return value[0, 0]


def own_entry(axis, size, first):
    entry, left = 0, size
    for stride, radix in groups_of(size, first):
        left //= radix
        entry = entry + digit_of(axis, stride, radix) * left
    return entry


def gather_all(value, axis, size, first):
    value = value[None]
    for stride, radix in reversed(groups_of(size, first)):
        digit = digit_of(axis, stride, radix)
        got = [value] + [swap(value, axis, size, stride * j) for j in range(1, radix)]
        whole = jnp.zeros((radix,) + value.shape, value.dtype)
        for j in range(radix):
            whole = lax.dynamic_update_index_in_dim(whole, got[j], digit ^ j, 0)
        value = whole.reshape((-1,) + value.shape[1:])
    return value


def body_large(samp, proto, embeddings, prototypes):
    per_view = embeddings.shape[1]
    width = embeddings.shape[2]
    unit_emb, inverse_emb = normalize_rows(embeddings)
    unit_proto, inverse_proto = normalize_rows(prototypes)
    emb_b = unit_emb.astype(jnp.bfloat16)
    proto_b = unit_proto.astype(jnp.bfloat16)
    scores = jnp.einsum("vbd,kd->vbk", emb_b, proto_b, preferred_element_type=jnp.float32)
    sink_exp = jnp.exp(scores / EPS_SINK)
    soft_exp = jnp.exp(scores / TEMPER)
    weights = jnp.ones((2, per_view), jnp.float32)
    proto_scale = jnp.ones((2, scores.shape[2]), jnp.float32)
    soft_total = weights
    cross_total = weights
    for sweep in range(ITERS):
        column_sums = jnp.sum(sink_exp * weights[:, :, None], axis=1)
        proto_scale = 1.0 / sum_all(column_sums, "samp", samp)
        row_sums = jnp.sum(sink_exp * proto_scale[:, None, :], axis=2)
        extras = []
        if sweep == 0:
            extras.append(jnp.sum(soft_exp, axis=2))
        if sweep == ITERS - 1:
            scaled_swap = (sink_exp * proto_scale[:, None, :])[::-1]
            extras.append(jnp.sum(scaled_swap * scores, axis=2))
        totals = sum_all(jnp.stack([row_sums] + extras), "proto", proto)
        weights = 1.0 / totals[0]
        if sweep == 0:
            soft_total = totals[1]
        if sweep == ITERS - 1:
            cross_total = totals[len(extras)]
    loss = jnp.log(soft_total) - cross_total * weights[::-1] / TEMPER
    assign = sink_exp * proto_scale[:, None, :] * weights[:, :, None]
    softmax_p = soft_exp / soft_total[:, :, None]
    slope_bf = ((softmax_p - assign[::-1]) / TEMPER).astype(jnp.bfloat16)

    emb_part = jnp.einsum("vbk,kd->vbd", slope_bf, proto_b, preferred_element_type=jnp.float32)
    rows = per_view // proto
    emb_part = emb_part.reshape(2, proto, rows, width).transpose(1, 0, 2, 3)
    emb_grad = scatter_sum(emb_part, "proto", proto, 2)
    entry = own_entry("proto", proto, 2)
    own_unit = lax.dynamic_slice_in_dim(unit_emb, entry * rows, rows, 1)
    own_inverse = lax.dynamic_slice_in_dim(inverse_emb, entry * rows, rows, 1)
    own_embed = project(emb_grad, own_unit, own_inverse).astype(jnp.bfloat16)

    proto_part = jnp.einsum("vbk,vbd->kd", slope_bf, emb_b, preferred_element_type=jnp.float32)
    lines = prototypes.shape[0] // samp
    proto_grad = scatter_sum(proto_part.reshape(samp, lines, width), "samp", samp, RADIX)
    entry = own_entry("samp", samp, RADIX)
    own_unit = lax.dynamic_slice_in_dim(unit_proto, entry * lines, lines, 0)
    own_inverse = lax.dynamic_slice_in_dim(inverse_proto, entry * lines, lines, 0)
    own_proto = project(proto_grad, own_unit, own_inverse).astype(jnp.bfloat16)

    grad_proto = gather_all(own_proto, "samp", samp, RADIX).reshape(prototypes.shape)
    grad_embed = gather_all(own_embed, "proto", proto, 2)
    grad_embed = grad_embed.transpose(1, 0, 2, 3).reshape(embeddings.shape)
    return (grad_embed, grad_proto, loss)


def dot_t(a, b):
    return lax.dot_general(a, b, (((1,), (1,)), ((), ())), preferred_element_type=jnp.float32)


def dot_n(a, b):
    return lax.dot_general(a, b, (((1,), (0,)), ((), ())), preferred_element_type=jnp.float32)


def unit_kernel(*refs):
    half = len(refs) // 2
    for raw_ref, out_ref in zip(refs[:half], refs[half:]):
        out_ref[...] = normalize_rows(raw_ref[...])[0].astype(jnp.bfloat16)


def score_kernel(tile, emb_ref, proto_ref, sink_ref, *sum_refs):
    rows = emb_ref.shape[0] // 2
    for view in range(2):
        emb = emb_ref[view * rows:(view + 1) * rows]
        total = jnp.zeros((8, rows), jnp.float32)
        for at in range(0, proto_ref.shape[0], tile):
            soft = jnp.exp2(dot_t(proto_ref[at:at + tile], emb) * (LOG2E / TEMPER))
            sink = soft * soft
            sink_ref[view, at:at + tile] = sink
            if sum_refs:
                total = total + jnp.sum(soft.reshape(-1, 8, rows), axis=0)
                lanes = sum(sink[:, lane:lane + 128] for lane in range(0, rows, 128))
                sum_refs[1][view:view + 1, at:at + tile] = jnp.sum(lanes.T, axis=0, keepdims=True)
        if sum_refs:
            sum_refs[0][view:view + 1] = jnp.sum(total, axis=0, keepdims=True)


def spread(weight_ref, view):
    lines = [weight_ref[2 * at + view:2 * at + view + 1] for at in range(4)]
    return [jnp.broadcast_to(line, (8, line.shape[1])) for line in lines]


def lane_sums(weight, block, view, part):
    values = block[view, part]
    tile, rows = values.shape
    scaled = (values.reshape(-1, 8, rows) * weight).reshape(tile, rows)
    return sum(scaled[:, lane:lane + 128] for lane in range(0, rows, 128))


def column_kernel(tile, weight_ref, own_ref, one_ref, two_ref, out_ref):
    for view in range(2):
        weight = spread(weight_ref, view)
        for first in range(0, own_ref.shape[1], tile):
            part = slice(first, first + tile)
            own, one, two = (lane_sums(weight[at], block, view, part) for at, block in enumerate((own_ref, one_ref, two_ref)))
            out_ref[0, view, part] = own + one
            out_ref[1, view, part] = two


def sweep_kernel(last, tile, weight_ref, own_ref, one_ref, two_ref, three_ref, *refs):
    out_ref = refs[-1]
    blocks = (own_ref, one_ref, two_ref, three_ref)
    _, count, rows = own_ref.shape
    if last:
        cross = [jnp.zeros((8, rows), jnp.float32)] * 2
        out_ref[...] = jnp.zeros(out_ref.shape, jnp.float32)
    for view in range(2):
        weight = spread(weight_ref, view)
        totals = [jnp.zeros((8, rows), jnp.float32)] * 4
        for first in range(0, count, tile):
            part = slice(first, first + tile)
            if last:
                lanes = [lane_sums(weight[at], blocks[at], view, part) for at in range(4)]
            else:
                lanes = [refs[0][0, view, part], refs[0][1, view, part] + lane_sums(weight[3], three_ref, view, part)]
            scale = 1.0 / jnp.sum(tree_sum(lanes), axis=1, keepdims=True)
            for at in range(4):
                scaled = blocks[at][view, part] * scale
                totals[at] = totals[at] + jnp.sum(scaled.reshape(-1, 8, rows), axis=0)
                if last and at == 0:
                    scaled = scaled * (jnp.log(own_ref[1 - view, part]) * EPS_SINK)
                    cross[1 - view] = cross[1 - view] + jnp.sum(scaled.reshape(-1, 8, rows), axis=0)
            if last:
                line = 10 + 2 * view + first // rows
                out_ref[line:line + 1, first % rows:first % rows + tile] = jnp.broadcast_to(scale, (tile, 128)).T[:1]
        for at in range(4):
            out_ref[2 * at + view:2 * at + view + 1] = jnp.sum(totals[at], axis=0, keepdims=True)
    if last:
        for view in range(2):
            out_ref[8 + view:9 + view] = jnp.sum(cross[view], axis=0, keepdims=True)


def found_kernel(mine_ref, theirs_ref, soft_ref, out_ref):
    totals = mine_ref[:10] + theirs_ref[:10]
    weights = 1.0 / totals[:8]
    soft = soft_ref[...]
    for view in range(2):
        crossed = totals[8 + view:9 + view] * weights[1 - view:2 - view]
        out_ref[view:view + 1] = jnp.log(soft[view:view + 1]) - crossed / TEMPER
    out_ref[2:10] = mine_ref[10:18]
    out_ref[10:18] = theirs_ref[10:18]
    out_ref[18:26] = weights / TEMPER
    out_ref[26:34] = 1.0 / (TEMPER * soft)


def finish(summed, raw):
    unit, inverse = normalize_rows(raw)
    return project(summed, unit, inverse).astype(jnp.bfloat16)


def column(row):
    return jnp.broadcast_to(row, (128, row.shape[1])).T


def widen(col, lanes):
    return jnp.concatenate([col] * (lanes // 128), axis=1)


def scale_row(found_ref, block, view, half):
    line = 2 + 4 * block + 2 * view + half
    return found_ref[line:line + 1]


def weight_row(found_ref, block, view):
    line = 18 + 2 * block + view
    return found_ref[line:line + 1]


def soft_row(found_ref, block, view):
    line = 26 + 2 * block + view
    return found_ref[line:line + 1]


def pipeline(steps, products_of, factors_of, place, soft_ref, slope_ref, rows):
    def slopes(step, first, last):
        slot = step % 2
        own_of, other_of = factors_of(step)
        for at in range(first, last, 16):
            part = slice(at, at + 16)
            soft = [jnp.exp2(soft_ref[(slot,) + place(view, part)] * (LOG2E / TEMPER)) for view in range(2)]
            taken = [other_of(view, part, soft[view] * soft[view]) for view in range(2)]
            for view in range(2):
                slope = own_of(view, part, soft[view]) - taken[1 - view]
                slope_ref[(slot,) + place(view, part)] = slope.astype(jnp.bfloat16)

    for step in range(-1, steps + 1):
        products = products_of(step + 1 if step + 1 < steps else None, step - 1 if step >= 1 else None)
        cuts = [rows * at // len(products) // 16 * 16 for at in range(len(products) + 1)]
        for at, product in enumerate(products):
            product()
            if 0 <= step < steps:
                slopes(step, cuts[at], cuts[at + 1])


def fetch_rows(sources, rows_ref, sem_ref):
    fetches = [pltpu.make_async_copy(source, rows_ref.at[at], sem_ref.at[at]) for at, source in enumerate(sources)]
    for fetch in fetches:
        fetch.start()
    return fetches


def proto_grad_kernel(tile, own_ref, one_ref, two_ref, three_ref, proto_ref, raw_ref, lead_raw_ref, found_ref,
                      out_ref, loss_ref, col_ref, acc_ref, work_ref, slope_ref, rows_ref, sem_ref):
    fetches = fetch_rows((raw_ref, lead_raw_ref), rows_ref, sem_ref)
    loss_ref[...] = found_ref[:2]
    blocks = (own_ref, one_ref, two_ref, three_ref)
    rows = own_ref.shape[0] // 2
    halves = rows // tile
    for view in range(2):
        for first in range(0, proto_ref.shape[0], rows):
            col_ref[view, first:first + rows] = column(scale_row(found_ref, 0, view, first // rows))

    def emb(step, view):
        first = view * rows + step % halves * tile
        return blocks[step // halves][first:first + tile]

    def score(step, view):
        work_ref[step % 2, :, view * tile:(view + 1) * tile] = dot_t(proto_ref[...], emb(step, view))

    def gradient(step):
        grad = dot_n(slope_ref[step % 2], jnp.concatenate([emb(step, 0), emb(step, 1)]))
        if step % halves:
            grad = grad + acc_ref[step // halves]
        acc_ref[step // halves] = grad

    def products_of(ahead, behind):
        scores = [] if ahead is None else [functools.partial(score, ahead, view) for view in range(2)]
        grads = [] if behind is None else [functools.partial(gradient, behind)]
        return scores[:1] + grads + scores[1:]

    def factors_of(step):
        block, first = step // halves, step % halves * tile
        part = slice(first, first + tile)
        soft = [jnp.broadcast_to(soft_row(found_ref, block, view)[:, part], (16, tile)) for view in range(2)]
        weight = [jnp.broadcast_to(weight_row(found_ref, block, view)[:, part], (16, tile)) for view in range(2)]

        def other_of(view, part, sink):
            return sink * widen(col_ref[view, part], tile) * weight[view]

        return (lambda view, part, value: value * soft[view]), other_of

    def place(view, part):
        return part, slice(view * tile, (view + 1) * tile)

    pipeline(len(blocks) * halves, products_of, factors_of, place, work_ref, slope_ref, proto_ref.shape[0])
    half = raw_ref.shape[0]
    for at in range(2):
        part = slice(at * half, (at + 1) * half)
        fetches[at].wait()
        out_ref[at] = finish(tree_sum([acc_ref[block, part] for block in range(4)]), rows_ref[at])


def emb_grad_kernel(tile, own_ref, one_ref, two_ref, three_ref, emb_ref, raw_ref, found_ref,
                    out_ref, loss_ref, col_ref, acc_ref, work_ref, slope_ref, rows_ref, sem_ref):
    fetches = fetch_rows((raw_ref.at[0], raw_ref.at[1]), rows_ref, sem_ref)
    loss_ref[...] = found_ref[:2]
    blocks = (own_ref, one_ref, two_ref, three_ref)
    rows = emb_ref.shape[0] // 2
    tiles = own_ref.shape[0] // tile
    for view in range(2):
        col_ref[view] = column(soft_row(found_ref, 0, view))
        col_ref[2 + view] = column(weight_row(found_ref, 0, view))

    def score(step, at):
        first = step % tiles * tile + at
        work_ref[step % 2, :, at:at + 256] = dot_t(emb_ref[...], blocks[step // tiles][first:first + 256])

    def gradient(step):
        block, first = step // tiles, step % tiles * tile
        grad = dot_n(slope_ref[step % 2], blocks[block][first:first + tile])
        if step % tiles:
            grad = grad + acc_ref[block]
        acc_ref[block] = grad

    def products_of(ahead, behind):
        scores = [] if ahead is None else [functools.partial(score, ahead, at) for at in range(0, tile, 256)]
        grads = [] if behind is None else [functools.partial(gradient, behind)]
        return scores[:1] + grads + scores[1:]

    def factors_of(step):
        block, half = step // tiles, step % tiles
        scale = [jnp.broadcast_to(scale_row(found_ref, block, view, half), (16, tile)) for view in range(2)]

        def own_of(view, part, value):
            return value * widen(col_ref[view, part], tile)

        def other_of(view, part, sink):
            return sink * scale[view] * widen(col_ref[2 + view, part], tile)

        return own_of, other_of

    def place(view, part):
        return (slice(view * rows + part.start, view * rows + part.stop),)

    pipeline(len(blocks) * tiles, products_of, factors_of, place, work_ref, slope_ref, rows)
    for view in range(2):
        part = slice(view * rows, (view + 1) * rows)
        total = tree_sum([acc_ref[block, part] for block in range(len(blocks))])
        fetches[view].wait()
        out_ref[view] = finish(total, rows_ref[view])


def own_part_kernel(core_ref, mine_ref, embed_ref, proto_ref, sem_ref):
    @pl.when(core_ref[0] == 0)
    def _():
        copy = pltpu.make_async_copy(mine_ref, embed_ref, sem_ref)
        copy.start()
        copy.wait()

    @pl.when(core_ref[0] == 1)
    def _():
        copy = pltpu.make_async_copy(mine_ref.at[1], proto_ref, sem_ref)
        copy.start()
        copy.wait()


def other_part_kernel(core_ref, theirs_ref, embed_in_ref, proto_in_ref, embed_ref, proto_ref, sem_ref):
    @pl.when(core_ref[0] == 0)
    def _():
        copy = pltpu.make_async_copy(theirs_ref.at[0], proto_ref, sem_ref)
        copy.start()
        copy.wait()

    @pl.when(core_ref[0] == 1)
    def _():
        copy = pltpu.make_async_copy(theirs_ref, embed_ref, sem_ref)
        copy.start()
        copy.wait()


def chip_masks(size, bits):
    return [bits << i for i in range((size // bits).bit_length() - 1)]


def chip_sum(value, axis, size, bits):
    for mask in chip_masks(size, bits):
        value = value + swap(value, axis, size, mask)
    return value


def chip_gather(value, axis, size, bits):
    value = value[None]
    for mask in chip_masks(size, bits):
        value = jnp.concatenate([value, swap(value, axis, size, mask)])
    return value


def scored(flat, proto_b, sums):
    rows, width = flat.shape
    count = proto_b.shape[0]
    shapes = [(2, count, rows // 2)] + [(2, rows // 2), (2, count)] * sums
    return pl.pallas_call(
        functools.partial(score_kernel, min(count, 256)),
        out_shape=[jax.ShapeDtypeStruct(shape, jnp.float32) for shape in shapes],
        in_specs=[VMEM] * 2,
        out_specs=[VMEM] * len(shapes),
        compiler_params=SMALL,
        cost_estimate=pl.CostEstimate(
            flops=2 * rows * count * width, bytes_accessed=2 * (rows + count) * width, transcendentals=rows * count
        ),
    )(flat, proto_b)


def swept(weights, sinks, *sums):
    _, count, rows = sinks[0].shape
    return pl.pallas_call(
        functools.partial(sweep_kernel, not sums, 128),
        out_shape=jax.ShapeDtypeStruct((8 if sums else 16, rows), jnp.float32),
        in_specs=[VMEM] * (5 + len(sums)),
        out_specs=VMEM,
        compiler_params=SMALL,
        cost_estimate=pl.CostEstimate(flops=32 * rows * count, bytes_accessed=4 * rows * count, transcendentals=0),
    )(weights, *sinks, *sums)


def first_sums(weights, sinks):
    _, count, rows = sinks[0].shape
    return pl.pallas_call(
        functools.partial(column_kernel, 128),
        out_shape=jax.ShapeDtypeStruct((2, 2, count, 128), jnp.float32),
        in_specs=[VMEM] * 4,
        out_specs=VMEM,
        compiler_params=SMALL,
        cost_estimate=pl.CostEstimate(flops=12 * rows * count, bytes_accessed=4 * rows * count, transcendentals=0),
    )(weights, *sinks[:3])


def after(value, first):
    return lax.optimization_barrier((value, first))


def sweeps(samp, proto, flat, own, other):
    proto_b = jnp.concatenate([other, own])
    sink, soft, sums = scored(flat, proto_b, True)
    sums = sums + swap(sums, "samp", samp, 1)
    block, sums = after(flat, sums)
    one = swap(block, "samp", samp, 1)
    two = swap(block, "samp", samp, 2)
    sums = sums + swap(sums, "samp", samp, 2)
    sums = jnp.concatenate([jnp.sum(sink * (1.0 / sums)[:, :, None], axis=1), soft])
    sums = sums + swap(sums, "proto", proto, 2)
    sums = sums + swap(sums, "proto", proto, 4)
    one, two, sums = lax.optimization_barrier((one, two, sums))
    half = one.shape[0] // 2
    three = jnp.concatenate([swap(one[:half], "samp", samp, 2), swap(two[half:], "samp", samp, 1)])

    both = jnp.concatenate([sums, swap(sums, "samp", samp, 2)])
    near, far = after(one, both)[0], after(two, both)[0]
    sinks = [sink] + [scored(block, proto_b, False)[0] for block in (near, far, three)]
    sums = jnp.concatenate([both, swap(both, "samp", samp, 1)])
    weights = 1.0 / jnp.concatenate([sums[at:at + 2] for at in (0, 8, 4, 12)])
    soft_total = jnp.concatenate([sums[at:at + 2] for at in (2, 10, 6, 14)])
    totals = chip_sum(swept(weights, sinks, first_sums(weights, sinks)), "proto", proto, 2)
    totals = swept(1.0 / totals, sinks)
    got = swap(totals, "proto", proto, 2)
    totals = jnp.concatenate([totals[:10] + got[:10], totals[10:14], got[10:14]])
    found = pl.pallas_call(
        found_kernel,
        out_shape=jax.ShapeDtypeStruct((34, flat.shape[0] // 2), jnp.float32),
        in_specs=[VMEM] * 3,
        out_specs=VMEM,
        compiler_params=SMALL,
    )(totals, swap(totals, "proto", proto, 4), soft_total)
    return found, one, two, three


def gathers(proto, flat, own, other):
    proto_b = jnp.concatenate([own, other])

    def middle(value):
        return lax.ppermute(value, "proto", [(2, 4), (4, 2)])

    one = swap(proto_b, "proto", proto, 2)
    near = middle(proto_b)
    far = middle(one)
    outer_near = swap(near, "proto", proto, 2)
    outer_far = swap(far, "proto", proto, 2)
    chip = lax.axis_index("proto") // 2
    inner = (chip == 1) | (chip == 2)
    two = jnp.where(inner, far, outer_near)
    three = jnp.where(inner, near, outer_far)
    return jnp.zeros((34, flat.shape[0] // 2), jnp.float32), one, two, three


def unit_rows(*raws):
    return pl.pallas_call(
        unit_kernel,
        out_shape=[jax.ShapeDtypeStruct(raw.shape, jnp.bfloat16) for raw in raws],
        in_specs=[VMEM] * len(raws),
        out_specs=[VMEM] * len(raws),
        compiler_params=SMALL,
    )(*raws)


def body(samp, proto, embeddings, prototypes):
    _, per_view, width = embeddings.shape
    count = prototypes.shape[0]
    core = lax.axis_index("proto") % 2
    lead = core == 1
    raw_other = swap(prototypes, "proto", proto, 1)
    flat, own = unit_rows(embeddings.reshape(2 * per_view, width), prototypes)
    other, = unit_rows(raw_other)
    raw_other = swap(after(prototypes, own)[0], "proto", proto, 1)
    found, *gathered = lax.cond(
        lead, functools.partial(sweeps, samp, proto), functools.partial(gathers, proto), flat, own, other
    )
    taken = swap(found, "proto", proto, 1)
    tile = min(2 * count, 512)

    def grads(kernel, operands, raws, columns, rows, lanes):
        return pl.pallas_call(
            functools.partial(kernel, lanes // 2 if kernel is proto_grad_kernel else lanes),
            out_shape=(
                jax.ShapeDtypeStruct((2, per_view, width), jnp.bfloat16),
                jax.ShapeDtypeStruct((2, per_view), jnp.float32),
            ),
            in_specs=[VMEM] * len(operands) + [HBM] * len(raws) + [VMEM],
            out_specs=(VMEM,) * 2,
            scratch_shapes=[
                pltpu.VMEM(columns, jnp.float32),
                pltpu.VMEM((4, 2 * count, width), jnp.float32),
                pltpu.VMEM((2, rows, lanes), jnp.float32),
                pltpu.VMEM((2, rows, lanes), jnp.bfloat16),
                pltpu.VMEM((2, per_view, width), jnp.bfloat16),
                pltpu.SemaphoreType.DMA((2,)),
            ],
            compiler_params=PARAMS,
        )(*operands, *raws, found if kernel is proto_grad_kernel else taken)[::-1]

    def proto_grads(flat, own, other, *gathered):
        proto_b = jnp.concatenate([other, own])
        operands = (flat, *gathered, proto_b)
        return grads(proto_grad_kernel, operands, (raw_other, prototypes), (2, 2 * count, 128), 2 * count, per_view)

    def emb_grads(flat, own, other, *gathered):
        proto_b = jnp.concatenate([own, other])
        operands = (proto_b, *gathered, flat)
        return grads(emb_grad_kernel, operands, (embeddings,), (4, per_view, 128), 2 * per_view, tile)

    loss, mine = lax.cond(lead, proto_grads, emb_grads, flat, own, other, *gathered)
    theirs = swap(mine, "proto", proto, 1)
    outputs = (
        jax.ShapeDtypeStruct(embeddings.shape, jnp.bfloat16),
        jax.ShapeDtypeStruct(prototypes.shape, jnp.bfloat16),
    )
    half_done = pl.pallas_call(
        own_part_kernel,
        out_shape=outputs,
        in_specs=[SMEM, ANY],
        out_specs=(ANY, ANY),
        scratch_shapes=[pltpu.SemaphoreType.DMA],
        compiler_params=SMALL,
    )(core.reshape(1), mine)
    grad_embed, grad_proto = pl.pallas_call(
        other_part_kernel,
        out_shape=outputs,
        in_specs=[SMEM, ANY, ANY, ANY],
        out_specs=(ANY, ANY),
        scratch_shapes=[pltpu.SemaphoreType.DMA],
        input_output_aliases={2: 0, 3: 1},
        compiler_params=SMALL,
    )(core.reshape(1), theirs, *half_done)
    return grad_embed, grad_proto, loss


def solution(mesh):
    samp, proto = mesh.shape["samp"], mesh.shape["proto"]

    def run(embeddings, prototypes):
        paired = samp == 4 and proto == 8 and prototypes.shape[0] == embeddings.shape[1] == 512
        return (body if paired else body_large)(samp, proto, embeddings, prototypes)

    return jax.shard_map(
        run,
        mesh=mesh,
        in_specs=(P(None, "samp", None), P("proto", None)),
        out_specs=(P(None, "samp", None), P("proto", None), P(None, "samp")),
        check_vma=False,
    )
```

```python
import functools
import math

import jax
import jax.numpy as jnp
from jax import lax
from jax.experimental import pallas as pl
from jax.experimental.pallas import tpu as pltpu
from jax.sharding import PartitionSpec as P

ITERS = 3


EPS_SINK = 0.05
TEMPER = 0.1
RADIX = 8
STEP = 2
LOG2E = math.log2(math.e)
VMEM = pl.BlockSpec(memory_space=pltpu.VMEM)
SMEM = pl.BlockSpec(memory_space=pltpu.SMEM)
ANY = pl.BlockSpec(memory_space=pl.ANY)
HBM = pl.BlockSpec(memory_space=pltpu.HBM)
PARAMS = pltpu.CompilerParams(vmem_limit_bytes=24 << 20)
SMALL = pltpu.CompilerParams(vmem_limit_bytes=8 << 20)


def normalize_rows(values):
    as_float = values.astype(jnp.float32)
    inverse = lax.rsqrt(jnp.sum(as_float * as_float, axis=-1, keepdims=True) + 1e-06)
    return (as_float * inverse, inverse)


def project(summed, unit_rows, inverse):
    return (summed - unit_rows * jnp.sum(unit_rows * summed, axis=-1, keepdims=True)) * inverse


def groups_of(size, first, later=RADIX):
    found, stride, limit = [], 1, first
    while stride < size:
        radix = min(limit, size // stride)
        found.append((stride, radix))
        stride, limit = stride * radix, later
    return found


def swap(value, axis, size, mask):
    return lax.ppermute(value, axis, [(i, i ^ mask) for i in range(size)])


def tree_sum(parts):
    while len(parts) > 1:
        parts = [parts[i] + parts[i + 1] for i in range(0, len(parts), 2)]
    return parts[0]


def sum_all(value, axis, size):
    for stride, radix in groups_of(size, STEP, STEP):
        value = tree_sum([value] + [swap(value, axis, size, stride * j) for j in range(1, radix)])
    return value


def digit_of(axis, stride, radix):
    return (lax.axis_index(axis) // stride) % radix


def scatter_sum(value, axis, size, first):
    value = value[None]
    for stride, radix in groups_of(size, first):
        digit = digit_of(axis, stride, radix)
        value = value.reshape((radix, -1) + value.shape[2:]) if value.shape[0] == 1 else value
        parts = [lax.dynamic_index_in_dim(value, digit ^ j, 0, keepdims=False) for j in range(radix)]
        got = [parts[0]] + [swap(parts[j], axis, size, stride * j) for j in range(1, radix)]
        value = tree_sum(got)[None]
    return value[0, 0]


def own_entry(axis, size, first):
    entry, left = 0, size
    for stride, radix in groups_of(size, first):
        left //= radix
        entry = entry + digit_of(axis, stride, radix) * left
    return entry


def gather_all(value, axis, size, first):
    value = value[None]
    for stride, radix in reversed(groups_of(size, first)):
        digit = digit_of(axis, stride, radix)
        got = [value] + [swap(value, axis, size, stride * j) for j in range(1, radix)]
        whole = jnp.zeros((radix,) + value.shape, value.dtype)
        for j in range(radix):
            whole = lax.dynamic_update_index_in_dim(whole, got[j], digit ^ j, 0)
        value = whole.reshape((-1,) + value.shape[1:])
    return value


def body_large(samp, proto, embeddings, prototypes):
    per_view = embeddings.shape[1]
    width = embeddings.shape[2]
    unit_emb, inverse_emb = normalize_rows(embeddings)
    unit_proto, inverse_proto = normalize_rows(prototypes)
    emb_b = unit_emb.astype(jnp.bfloat16)
    proto_b = unit_proto.astype(jnp.bfloat16)
    scores = jnp.einsum("vbd,kd->vbk", emb_b, proto_b, preferred_element_type=jnp.float32)
    sink_exp = jnp.exp(scores / EPS_SINK)
    soft_exp = jnp.exp(scores / TEMPER)
    weights = jnp.ones((2, per_view), jnp.float32)
    proto_scale = jnp.ones((2, scores.shape[2]), jnp.float32)
    soft_total = weights
    cross_total = weights
    for sweep in range(ITERS):
        column_sums = jnp.sum(sink_exp * weights[:, :, None], axis=1)
        proto_scale = 1.0 / sum_all(column_sums, "samp", samp)
        row_sums = jnp.sum(sink_exp * proto_scale[:, None, :], axis=2)
        extras = []
        if sweep == 0:
            extras.append(jnp.sum(soft_exp, axis=2))
        if sweep == ITERS - 1:
            scaled_swap = (sink_exp * proto_scale[:, None, :])[::-1]
            extras.append(jnp.sum(scaled_swap * scores, axis=2))
        totals = sum_all(jnp.stack([row_sums] + extras), "proto", proto)
        weights = 1.0 / totals[0]
        if sweep == 0:
            soft_total = totals[1]
        if sweep == ITERS - 1:
            cross_total = totals[len(extras)]
    loss = jnp.log(soft_total) - cross_total * weights[::-1] / TEMPER
    assign = sink_exp * proto_scale[:, None, :] * weights[:, :, None]
    softmax_p = soft_exp / soft_total[:, :, None]
    slope_bf = ((softmax_p - assign[::-1]) / TEMPER).astype(jnp.bfloat16)

    emb_part = jnp.einsum("vbk,kd->vbd", slope_bf, proto_b, preferred_element_type=jnp.float32)
    rows = per_view // proto
    emb_part = emb_part.reshape(2, proto, rows, width).transpose(1, 0, 2, 3)
    emb_grad = scatter_sum(emb_part, "proto", proto, 2)
    entry = own_entry("proto", proto, 2)
    own_unit = lax.dynamic_slice_in_dim(unit_emb, entry * rows, rows, 1)
    own_inverse = lax.dynamic_slice_in_dim(inverse_emb, entry * rows, rows, 1)
    own_embed = project(emb_grad, own_unit, own_inverse).astype(jnp.bfloat16)

    proto_part = jnp.einsum("vbk,vbd->kd", slope_bf, emb_b, preferred_element_type=jnp.float32)
    lines = prototypes.shape[0] // samp
    proto_grad = scatter_sum(proto_part.reshape(samp, lines, width), "samp", samp, RADIX)
    entry = own_entry("samp", samp, RADIX)
    own_unit = lax.dynamic_slice_in_dim(unit_proto, entry * lines, lines, 0)
    own_inverse = lax.dynamic_slice_in_dim(inverse_proto, entry * lines, lines, 0)
    own_proto = project(proto_grad, own_unit, own_inverse).astype(jnp.bfloat16)

    grad_proto = gather_all(own_proto, "samp", samp, RADIX).reshape(prototypes.shape)
    grad_embed = gather_all(own_embed, "proto", proto, 2)
    grad_embed = grad_embed.transpose(1, 0, 2, 3).reshape(embeddings.shape)
    return (grad_embed, grad_proto, loss)


def dot_t(a, b):
    return lax.dot_general(a, b, (((1,), (1,)), ((), ())), preferred_element_type=jnp.float32)


def dot_n(a, b):
    return lax.dot_general(a, b, (((1,), (0,)), ((), ())), preferred_element_type=jnp.float32)


def unit_kernel(*refs):
    half = len(refs) // 2
    for raw_ref, out_ref in zip(refs[:half], refs[half:]):
        out_ref[...] = normalize_rows(raw_ref[...])[0].astype(jnp.bfloat16)


def score_kernel(tile, emb_ref, proto_ref, sink_ref, *sum_refs):
    rows = emb_ref.shape[0] // 2
    for view in range(2):
        emb = emb_ref[view * rows:(view + 1) * rows]
        total = jnp.zeros((8, rows), jnp.float32)
        for at in range(0, proto_ref.shape[0], tile):
            soft = jnp.exp2(dot_t(proto_ref[at:at + tile], emb) * (LOG2E / TEMPER))
            sink = soft * soft
            sink_ref[view, at:at + tile] = sink
            if sum_refs:
                total = total + jnp.sum(soft.reshape(-1, 8, rows), axis=0)
                lanes = sum(sink[:, lane:lane + 128] for lane in range(0, rows, 128))
                sum_refs[1][view:view + 1, at:at + tile] = jnp.sum(lanes.T, axis=0, keepdims=True)
        if sum_refs:
            sum_refs[0][view:view + 1] = jnp.sum(total, axis=0, keepdims=True)


def spread(weight_ref, view):
    lines = [weight_ref[2 * at + view:2 * at + view + 1] for at in range(4)]
    return [jnp.broadcast_to(line, (8, line.shape[1])) for line in lines]


def fetched_unit_kernel(pieces, *refs):
    raw_refs, out_refs, held_refs, sem_ref = refs[:2], refs[2:4], refs[4:6], refs[6]
    copies = []
    for raw_ref, out_ref, held_ref in zip(raw_refs, out_refs, held_refs):
        size = raw_ref.shape[0] // pieces
        for at in range(pieces):
            part = pl.ds(at * size, size)
            copy = pltpu.make_async_copy(raw_ref.at[part], held_ref.at[part], sem_ref.at[len(copies)])
            copy.start()
            copies.append((copy, held_ref, out_ref, part))
    for copy, held_ref, out_ref, part in copies:
        copy.wait()
        out_ref[part] = normalize_rows(held_ref[part])[0].astype(jnp.bfloat16)


def lane_sums(weight, block, view, part):
    values = block[view, part]
    tile, rows = values.shape
    scaled = (values.reshape(-1, 8, rows) * weight).reshape(tile, rows)
    return sum(scaled[:, lane:lane + 128] for lane in range(0, rows, 128))


def column_kernel(tile, weight_ref, own_ref, one_ref, two_ref, out_ref):
    for view in range(2):
        weight = spread(weight_ref, view)
        for first in range(0, own_ref.shape[1], tile):
            part = slice(first, first + tile)
            own, one, two = (lane_sums(weight[at], block, view, part) for at, block in enumerate((own_ref, one_ref, two_ref)))
            out_ref[0, view, part] = own + one
            out_ref[1, view, part] = two


def sweep_kernel(last, tile, weight_ref, own_ref, one_ref, two_ref, three_ref, *refs):
    out_ref = refs[-1]
    blocks = (own_ref, one_ref, two_ref, three_ref)
    _, count, rows = own_ref.shape
    for view in range(2):
        weight = spread(weight_ref, view)
        totals = [jnp.zeros((8, rows), jnp.float32)] * 4
        for first in range(0, count, tile):
            part = slice(first, first + tile)
            if last:
                lanes = [lane_sums(weight[at], blocks[at], view, part) for at in range(4)]
            else:
                lanes = [refs[0][0, view, part], refs[0][1, view, part] + lane_sums(weight[3], three_ref, view, part)]
            scale = 1.0 / jnp.sum(tree_sum(lanes), axis=1, keepdims=True)
            for at in range(4):
                scaled = blocks[at][view, part] * scale
                totals[at] = totals[at] + jnp.sum(scaled.reshape(-1, 8, rows), axis=0)
            if last:
                line = 8 + 2 * view + first // rows
                out_ref[line:line + 1, first % rows:first % rows + tile] = jnp.broadcast_to(scale, (tile, 128)).T[:1]
        for at in range(4):
            out_ref[2 * at + view:2 * at + view + 1] = jnp.sum(totals[at], axis=0, keepdims=True)


def pack_kernel(mine_ref, theirs_ref, out_ref):
    out_ref[:8] = mine_ref[:8] + theirs_ref[:8]
    out_ref[8:12] = mine_ref[8:12]
    out_ref[12:16] = theirs_ref[8:12]


def found_kernel(mine_ref, theirs_ref, soft_ref, out_ref):
    soft = soft_ref[...]
    out_ref[:2] = jnp.log(soft[:2])
    out_ref[2:10] = mine_ref[8:16]
    out_ref[10:18] = theirs_ref[8:16]
    out_ref[18:26] = 1.0 / (TEMPER * (mine_ref[:8] + theirs_ref[:8]))
    out_ref[26:34] = 1.0 / (TEMPER * soft)


def finish(summed, raw):
    unit, inverse = normalize_rows(raw)
    return project(summed, unit, inverse).astype(jnp.bfloat16)


def column(row):
    return jnp.broadcast_to(row, (128, row.shape[1])).T


def widen(col, lanes):
    return jnp.concatenate([col] * (lanes // 128), axis=1)


def scale_row(found_ref, block, view, half):
    line = 2 + 4 * block + 2 * view + half
    return found_ref[line:line + 1]


def weight_row(found_ref, block, view):
    line = 18 + 2 * block + view
    return found_ref[line:line + 1]


def soft_row(found_ref, block, view):
    line = 26 + 2 * block + view
    return found_ref[line:line + 1]


def pipeline(steps, products_of, factors_of, place, soft_ref, slope_ref, rows, cross_of=None):
    def slopes(step, first, last):
        slot = step % 2
        own_of, other_of = factors_of(step)
        for at in range(first, last, 16):
            part = slice(at, at + 16)
            scores = [soft_ref[(slot,) + place(view, part)] for view in range(2)]
            soft = [jnp.exp2(scores[view] * (LOG2E / TEMPER)) for view in range(2)]
            taken = [other_of(view, part, soft[view] * soft[view]) for view in range(2)]
            for view in range(2):
                slope = own_of(view, part, soft[view]) - taken[1 - view]
                if cross_of:
                    cross_of(step, view, part, scores[view] * taken[1 - view])
                slope_ref[(slot,) + place(view, part)] = slope.astype(jnp.bfloat16)

    for step in range(-1, steps + 1):
        products = products_of(step + 1 if step + 1 < steps else None, step - 1 if step >= 1 else None)
        cuts = [rows * at // len(products) // 16 * 16 for at in range(len(products) + 1)]
        for at, product in enumerate(products):
            product()
            if 0 <= step < steps:
                slopes(step, cuts[at], cuts[at + 1])


def fetch_rows(sources, rows_ref, sem_ref):
    fetches = [pltpu.make_async_copy(source, rows_ref.at[at], sem_ref.at[at]) for at, source in enumerate(sources)]
    for fetch in fetches:
        fetch.start()
    return fetches


def proto_grad_kernel(tile, own_ref, one_ref, two_ref, three_ref, proto_ref, raw_ref, lead_raw_ref, found_ref,
                      out_ref, loss_ref, col_ref, acc_ref, work_ref, slope_ref, rows_ref, sem_ref):
    fetches = fetch_rows((raw_ref, lead_raw_ref), rows_ref, sem_ref)
    loss_ref[...] = found_ref[:2]
    blocks = (own_ref, one_ref, two_ref, three_ref)
    rows = own_ref.shape[0] // 2
    halves = rows // tile
    for view in range(2):
        for first in range(0, proto_ref.shape[0], rows):
            col_ref[view, first:first + rows] = column(scale_row(found_ref, 0, view, first // rows))

    def emb(step, view):
        first = view * rows + step % halves * tile
        return blocks[step // halves][first:first + tile]

    def score(step, view):
        work_ref[step % 2, :, view * tile:(view + 1) * tile] = dot_t(proto_ref[...], emb(step, view))

    def gradient(step):
        grad = dot_n(slope_ref[step % 2], jnp.concatenate([emb(step, 0), emb(step, 1)]))
        if step % halves:
            grad = grad + acc_ref[step // halves]
        acc_ref[step // halves] = grad

    def products_of(ahead, behind):
        scores = [] if ahead is None else [functools.partial(score, ahead, view) for view in range(2)]
        grads = [] if behind is None else [functools.partial(gradient, behind)]
        return scores[:1] + grads + scores[1:]

    def factors_of(step):
        block, first = step // halves, step % halves * tile
        part = slice(first, first + tile)
        soft = [jnp.broadcast_to(soft_row(found_ref, block, view)[:, part], (16, tile)) for view in range(2)]
        weight = [jnp.broadcast_to(weight_row(found_ref, block, view)[:, part], (16, tile)) for view in range(2)]

        def other_of(view, part, sink):
            return sink * widen(col_ref[view, part], tile) * weight[view]

        return (lambda view, part, value: value * soft[view]), other_of

    def place(view, part):
        return part, slice(view * tile, (view + 1) * tile)

    pipeline(len(blocks) * halves, products_of, factors_of, place, work_ref, slope_ref, proto_ref.shape[0])
    half = raw_ref.shape[0]
    for at in range(2):
        part = slice(at * half, (at + 1) * half)
        fetches[at].wait()
        out_ref[at] = finish(tree_sum([acc_ref[block, part] for block in range(4)]), rows_ref[at])


def emb_grad_kernel(tile, own_ref, one_ref, two_ref, three_ref, emb_ref, raw_ref, found_ref,
                    out_ref, loss_ref, col_ref, acc_ref, work_ref, slope_ref, rows_ref, sem_ref, cross_ref):
    fetches = fetch_rows((raw_ref.at[0], raw_ref.at[1]), rows_ref, sem_ref)
    blocks = (own_ref, one_ref, two_ref, three_ref)
    rows = emb_ref.shape[0] // 2
    tiles = own_ref.shape[0] // tile
    for view in range(2):
        col_ref[view] = column(soft_row(found_ref, 0, view))
        col_ref[2 + view] = column(weight_row(found_ref, 0, view))

    def score(step, at):
        first = step % tiles * tile + at
        work_ref[step % 2, :, at:at + 256] = dot_t(emb_ref[...], blocks[step // tiles][first:first + 256])

    def gradient(step):
        block, first = step // tiles, step % tiles * tile
        grad = dot_n(slope_ref[step % 2], blocks[block][first:first + tile])
        if step % tiles:
            grad = grad + acc_ref[block]
        acc_ref[block] = grad

    def products_of(ahead, behind):
        scores = [] if ahead is None else [functools.partial(score, ahead, at) for at in range(0, tile, 256)]
        grads = [] if behind is None else [functools.partial(gradient, behind)]
        return scores[:1] + grads + scores[1:]

    def factors_of(step):
        block, half = step // tiles, step % tiles
        scale = [jnp.broadcast_to(scale_row(found_ref, block, view, half), (16, tile)) for view in range(2)]

        def own_of(view, part, value):
            return value * widen(col_ref[view, part], tile)

        def other_of(view, part, sink):
            return sink * scale[view] * widen(col_ref[2 + view, part], tile)

        return own_of, other_of

    def place(view, part):
        return (slice(view * rows + part.start, view * rows + part.stop),)

    def cross_of(step, view, part, crossed):
        lanes = sum(crossed[:, lane:lane + 128] for lane in range(0, tile, 128))
        if step % tiles:
            lanes = lanes + cross_ref[step // tiles, view, part]
        cross_ref[step // tiles, view, part] = lanes

    pipeline(len(blocks) * tiles, products_of, factors_of, place, work_ref, slope_ref, rows, cross_of)
    for view in range(2):
        crossed = tree_sum([cross_ref[block, view] for block in range(len(blocks))])
        loss_ref[view:view + 1] = found_ref[view:view + 1] - jnp.sum(crossed.T, axis=0, keepdims=True)
        part = slice(view * rows, (view + 1) * rows)
        total = tree_sum([acc_ref[block, part] for block in range(len(blocks))])
        fetches[view].wait()
        out_ref[view] = finish(total, rows_ref[view])


def copy_all(pairs, sem_ref):
    copies = [pltpu.make_async_copy(source, target, sem_ref.at[at]) for at, (source, target) in enumerate(pairs)]
    for copy in copies:
        copy.start()
    for copy in copies:
        copy.wait()


def own_part_kernel(core_ref, mine_ref, made_ref, embed_ref, proto_ref, loss_ref, sem_ref):
    @pl.when(core_ref[0] == 0)
    def _():
        copy_all([(mine_ref, embed_ref), (made_ref, loss_ref)], sem_ref)

    @pl.when(core_ref[0] == 1)
    def _():
        copy_all([(mine_ref.at[1], proto_ref)], sem_ref)


def other_part_kernel(core_ref, theirs_ref, made_ref, embed_in_ref, proto_in_ref, loss_in_ref,
                      embed_ref, proto_ref, loss_ref, sem_ref):
    @pl.when(core_ref[0] == 0)
    def _():
        copy_all([(theirs_ref.at[0], proto_ref)], sem_ref)

    @pl.when(core_ref[0] == 1)
    def _():
        copy_all([(theirs_ref, embed_ref), (made_ref, loss_ref)], sem_ref)


def chip_masks(size, bits):
    return [bits << i for i in range((size // bits).bit_length() - 1)]


def chip_sum(value, axis, size, bits):
    for mask in chip_masks(size, bits):
        value = value + swap(value, axis, size, mask)
    return value


def chip_gather(value, axis, size, bits):
    value = value[None]
    for mask in chip_masks(size, bits):
        value = jnp.concatenate([value, swap(value, axis, size, mask)])
    return value


def scored(flat, proto_b, sums):
    rows, width = flat.shape
    count = proto_b.shape[0]
    shapes = [(2, count, rows // 2)] + [(2, rows // 2), (2, count)] * sums
    return pl.pallas_call(
        functools.partial(score_kernel, min(count, 256)),
        out_shape=[jax.ShapeDtypeStruct(shape, jnp.float32) for shape in shapes],
        in_specs=[VMEM] * 2,
        out_specs=[VMEM] * len(shapes),
        compiler_params=SMALL,
        cost_estimate=pl.CostEstimate(
            flops=2 * rows * count * width, bytes_accessed=2 * (rows + count) * width, transcendentals=rows * count
        ),
    )(flat, proto_b)


def swept(weights, sinks, *sums):
    _, count, rows = sinks[0].shape
    return pl.pallas_call(
        functools.partial(sweep_kernel, not sums, 128),
        out_shape=jax.ShapeDtypeStruct((8 if sums else 12, rows), jnp.float32),
        in_specs=[VMEM] * (5 + len(sums)),
        out_specs=VMEM,
        compiler_params=SMALL,
        cost_estimate=pl.CostEstimate(flops=32 * rows * count, bytes_accessed=4 * rows * count, transcendentals=0),
    )(weights, *sinks, *sums)


def first_sums(weights, sinks):
    _, count, rows = sinks[0].shape
    return pl.pallas_call(
        functools.partial(column_kernel, 128),
        out_shape=jax.ShapeDtypeStruct((2, 2, count, 128), jnp.float32),
        in_specs=[VMEM] * 4,
        out_specs=VMEM,
        compiler_params=SMALL,
        cost_estimate=pl.CostEstimate(flops=12 * rows * count, bytes_accessed=4 * rows * count, transcendentals=0),
    )(weights, *sinks[:3])


def after(value, first):
    return lax.optimization_barrier((value, first))


def sweeps(samp, proto, flat, own, other):
    proto_b = jnp.concatenate([other, own])
    sink, soft, sums = scored(flat, proto_b, True)
    sums = sums + swap(sums, "samp", samp, 1)
    block, sums = after(flat, sums)
    one = swap(block, "samp", samp, 1)
    two = swap(block, "samp", samp, 2)
    sums = sums + swap(sums, "samp", samp, 2)
    sums = jnp.concatenate([jnp.sum(sink * (1.0 / sums)[:, :, None], axis=1), soft])
    sums = sums + swap(sums, "proto", proto, 2)
    sums = sums + swap(sums, "proto", proto, 4)
    one, two, sums = lax.optimization_barrier((one, two, sums))
    half = one.shape[0] // 2
    three = jnp.concatenate([swap(one[:half], "samp", samp, 2), swap(two[half:], "samp", samp, 1)])

    both = jnp.concatenate([sums, swap(sums, "samp", samp, 2)])
    near, far = after(one, both)[0], after(two, both)[0]
    sinks = [sink] + [scored(block, proto_b, False)[0] for block in (near, far, three)]
    sums = jnp.concatenate([both, swap(both, "samp", samp, 1)])
    weights = 1.0 / jnp.concatenate([sums[at:at + 2] for at in (0, 8, 4, 12)])
    soft_total = jnp.concatenate([sums[at:at + 2] for at in (2, 10, 6, 14)])
    totals = chip_sum(swept(weights, sinks, first_sums(weights, sinks)), "proto", proto, 2)
    totals = swept(1.0 / totals, sinks)
    totals = pl.pallas_call(
        pack_kernel,
        out_shape=jax.ShapeDtypeStruct((16, flat.shape[0] // 2), jnp.float32),
        in_specs=[VMEM] * 2,
        out_specs=VMEM,
        compiler_params=SMALL,
    )(totals, swap(totals, "proto", proto, 2))
    found = pl.pallas_call(
        found_kernel,
        out_shape=jax.ShapeDtypeStruct((34, flat.shape[0] // 2), jnp.float32),
        in_specs=[VMEM] * 3,
        out_specs=VMEM,
        compiler_params=SMALL,
    )(totals, swap(totals, "proto", proto, 4), soft_total)
    return found, one, two, three


def gathers(proto, flat, own, other):
    proto_b = jnp.concatenate([own, other])

    def middle(value):
        return lax.ppermute(value, "proto", [(2, 4), (4, 2)])

    one = swap(proto_b, "proto", proto, 2)
    near = middle(proto_b)
    far = middle(one)
    outer_near = swap(near, "proto", proto, 2)
    outer_far = swap(far, "proto", proto, 2)
    chip = lax.axis_index("proto") // 2
    inner = (chip == 1) | (chip == 2)
    two = jnp.where(inner, far, outer_near)
    three = jnp.where(inner, near, outer_far)
    return jnp.zeros((34, flat.shape[0] // 2), jnp.float32), one, two, three


def unit_rows(*raws):
    return pl.pallas_call(
        unit_kernel,
        out_shape=[jax.ShapeDtypeStruct(raw.shape, jnp.bfloat16) for raw in raws],
        in_specs=[VMEM] * len(raws),
        out_specs=[VMEM] * len(raws),
        compiler_params=SMALL,
    )(*raws)


def body(samp, proto, embeddings, prototypes):
    _, per_view, width = embeddings.shape
    count = prototypes.shape[0]
    core = lax.axis_index("proto") % 2
    lead = core == 1
    raw_other = swap(prototypes, "proto", proto, 1)
    raws = (prototypes, embeddings.reshape(2 * per_view, width))
    own, flat = pl.pallas_call(
        functools.partial(fetched_unit_kernel, 2),
        out_shape=[jax.ShapeDtypeStruct(raw.shape, jnp.bfloat16) for raw in raws],
        in_specs=[HBM] * 2,
        out_specs=[VMEM] * 2,
        scratch_shapes=[pltpu.VMEM(raw.shape, jnp.bfloat16) for raw in raws] + [pltpu.SemaphoreType.DMA((4,))],
        compiler_params=SMALL,
    )(*raws)
    other, = unit_rows(raw_other)
    raw_other = swap(after(prototypes, own)[0], "proto", proto, 1)
    found, *gathered = lax.cond(
        lead, functools.partial(sweeps, samp, proto), functools.partial(gathers, proto), flat, own, other
    )
    taken = swap(found, "proto", proto, 1)
    tile = min(2 * count, 512)

    def grads(kernel, operands, raws, columns, rows, lanes):
        return pl.pallas_call(
            functools.partial(kernel, lanes // 2 if kernel is proto_grad_kernel else lanes),
            out_shape=(
                jax.ShapeDtypeStruct((2, per_view, width), jnp.bfloat16),
                jax.ShapeDtypeStruct((2, per_view), jnp.float32),
            ),
            in_specs=[VMEM] * len(operands) + [HBM] * len(raws) + [VMEM],
            out_specs=(VMEM,) * 2,
            scratch_shapes=[
                pltpu.VMEM(columns, jnp.float32),
                pltpu.VMEM((4, 2 * count, width), jnp.float32),
                pltpu.VMEM((2, rows, lanes), jnp.float32),
                pltpu.VMEM((2, rows, lanes), jnp.bfloat16),
                pltpu.VMEM((2, per_view, width), jnp.bfloat16),
                pltpu.SemaphoreType.DMA((2,)),
            ] + [pltpu.VMEM((4, 2, per_view, 128), jnp.float32)] * (kernel is emb_grad_kernel),
            compiler_params=PARAMS,
        )(*operands, *raws, found if kernel is proto_grad_kernel else taken)[::-1]

    def proto_grads(flat, own, other, *gathered):
        proto_b = jnp.concatenate([other, own])
        operands = (flat, *gathered, proto_b)
        return grads(proto_grad_kernel, operands, (raw_other, prototypes), (2, 2 * count, 128), 2 * count, per_view)

    def emb_grads(flat, own, other, *gathered):
        proto_b = jnp.concatenate([own, other])
        operands = (proto_b, *gathered, flat)
        return grads(emb_grad_kernel, operands, (embeddings,), (4, per_view, 128), 2 * per_view, tile)

    loss, mine = lax.cond(lead, proto_grads, emb_grads, flat, own, other, *gathered)
    theirs = swap(mine, "proto", proto, 1)
    their_loss = swap(loss, "proto", proto, 1)
    outputs = (
        jax.ShapeDtypeStruct(embeddings.shape, jnp.bfloat16),
        jax.ShapeDtypeStruct(prototypes.shape, jnp.bfloat16),
        jax.ShapeDtypeStruct((2, per_view), jnp.float32),
    )
    half_done = pl.pallas_call(
        own_part_kernel,
        out_shape=outputs,
        in_specs=[SMEM, ANY, ANY],
        out_specs=(ANY,) * 3,
        scratch_shapes=[pltpu.SemaphoreType.DMA((2,))],
        compiler_params=SMALL,
    )(core.reshape(1), mine, loss)
    return pl.pallas_call(
        other_part_kernel,
        out_shape=outputs,
        in_specs=[SMEM] + [ANY] * 5,
        out_specs=(ANY,) * 3,
        scratch_shapes=[pltpu.SemaphoreType.DMA((2,))],
        input_output_aliases={3: 0, 4: 1, 5: 2},
        compiler_params=SMALL,
    )(core.reshape(1), theirs, their_loss, *half_done)


def solution(mesh):
    samp, proto = mesh.shape["samp"], mesh.shape["proto"]

    def run(embeddings, prototypes):
        paired = samp == 4 and proto == 8 and prototypes.shape[0] == embeddings.shape[1] == 512
        return (body if paired else body_large)(samp, proto, embeddings, prototypes)

    return jax.shard_map(
        run,
        mesh=mesh,
        in_specs=(P(None, "samp", None), P("proto", None)),
        out_specs=(P(None, "samp", None), P("proto", None), P(None, "samp")),
        check_vma=False,
    )
```
